128 devices in a mesh: dp: 32 (over x, y, z_lo), seq: 4 (over z_hi, core).
Axes of the slice: x: 4, y: 4, z: 4 (z_hi: 2, z_lo: 2; z = z_hi * 2 + z_lo), core: 2. Of those that a mesh axis runs over, the one named last changes fastest.
Arguments:
- block_in: bfloat16 [32, 1024, 768], P('dp', 'seq'), may hold values from -6 to 6
- cotangent: bfloat16 [32, 1024, 768], P('dp', 'seq'), may hold values from -6 to 6
- attn_gain: bfloat16 [768], P('dp'), may hold values from 0.099609375 to 1.8984375
- attn_bias: bfloat16 [768], P('dp'), may hold values from -3 to 3
- mlp_gain: bfloat16 [768], P('dp'), may hold values from 0.099609375 to 1.8984375
- mlp_bias: bfloat16 [768], P('dp'), may hold values from -3 to 3
- qkv_weight: bfloat16 [768, 2304], P('dp'), may hold values from -0.21875 to 0.21875
- qkv_bias: bfloat16 [2304], P('dp'), may hold values from -3 to 3
- proj_weight: bfloat16 [768, 768], P('dp'), may hold values from -2.5 to 2.5
- proj_bias: bfloat16 [768], P('dp'), may hold values from -3 to 3
- up_weight: bfloat16 [768, 3072], P('dp'), may hold values from -0.21875 to 0.21875
- up_bias: bfloat16 [3072], P('dp'), may hold values from -3 to 3
- down_weight: bfloat16 [3072, 768], P('dp'), may hold values from -0.109375 to 0.109375
- down_bias: bfloat16 [768], P('dp'), may hold values from -3 to 3
Outputs:
- block_out: bfloat16 [32, 1024, 768], P('dp', 'seq')
- input_grad: bfloat16 [32, 1024, 768], P('dp', 'seq')
- attn_gain_grad: float32 [768], P('dp')
- attn_bias_grad: float32 [768], P('dp')
- mlp_gain_grad: float32 [768], P('dp')
- mlp_bias_grad: float32 [768], P('dp')
- qkv_weight_grad: float32 [768, 2304], P('dp')
- qkv_bias_grad: float32 [2304], P('dp')
- proj_weight_grad: float32 [768, 768], P('dp')
- proj_bias_grad: float32 [768], P('dp')
- up_weight_grad: float32 [768, 3072], P('dp')
- up_bias_grad: float32 [3072], P('dp')
- down_weight_grad: float32 [3072, 768], P('dp')
- down_bias_grad: float32 [768], P('dp')
The draws below stay inside these ranges and needn't reach their ends.
All inputs are finite; a program needn't handle non-finite values.
Results may differ from the reference program's by a relative error of at most 0.025.
Values may be sent and summed in bfloat16 or wider, within the bound.
A program may use at most 128 MiB of HBM per device.

```python
import math
import jax
import jax.numpy as jnp
from jax import lax

D = 768
FF = 3072
HEADS = 12
HEAD_DIM = 64
ROT_DIM = 16
SEQ_LEN = 1024
SEQUENCES = 32


def levels(own_key, extent, pieces, least, top_value):
    level = 1.0
    for position, shards_of in pieces:
        heights = jax.random.uniform(jax.random.fold_in(jax.random.fold_in(own_key, 6), position), (shards_of,), jnp.float32, least / len(pieces), top_value / len(pieces))
        level = level * jnp.repeat(jnp.exp(heights), extent[position] // shards_of).reshape((-1,) + (1,) * (len(extent) - 1 - position))
    return level


def normal_values(rng, shape, deviation, reach, pieces=(), held_as=jnp.bfloat16):
    values = deviation * jax.random.normal(rng, shape, jnp.float32)
    if pieces:
        values = values * levels(rng, shape, pieces, -0.22, 0.18)
    return jnp.clip(values, -reach, reach).astype(held_as)


def setup_inputs(seed: int = 0) -> dict:
    streams_of = jax.random.split(jax.random.key(seed), 15)
    return {
        "block_in": normal_values(streams_of[0], (SEQUENCES, SEQ_LEN, D), 1.0, 6.0, ((0, 32), (1, 4))),
        "cotangent": normal_values(streams_of[1], (SEQUENCES, SEQ_LEN, D), 1.0, 6.0, ((0, 32), (1, 4))),
        "attn_gain": jnp.clip(1.0 + 0.18 * jax.random.normal(streams_of[2], (D,), jnp.float32), 0.099609375, 1.8984375).astype(jnp.bfloat16),
        "attn_bias": normal_values(streams_of[3], (D,), 0.3, 3.0, ((0, 32),)),
        "mlp_gain": jnp.clip(1.0 + 0.18 * jax.random.normal(streams_of[4], (D,), jnp.float32), 0.099609375, 1.8984375).astype(jnp.bfloat16),
        "mlp_bias": normal_values(streams_of[5], (D,), 0.3, 3.0, ((0, 32),)),
        "qkv_weight": normal_values(streams_of[6], (D, 3 * D), D ** -0.5, 0.21875, ((0, 32),)),
        "qkv_bias": normal_values(streams_of[7], (3 * D,), 0.3, 3.0, ((0, 32),)),
        "proj_weight": normal_values(streams_of[8], (D, D), (max(D * 8 // SEQ_LEN, 1)) ** -0.5, 2.5, ((0, 32),)),
        "proj_bias": normal_values(streams_of[9], (D,), 0.3, 3.0, ((0, 32),)),
        "up_weight": normal_values(streams_of[10], (D, FF), D ** -0.5, 0.21875, ((0, 32),)),
        "up_bias": normal_values(streams_of[11], (FF,), 0.5, 3.0, ((0, 32),)),
        "down_weight": normal_values(streams_of[12], (FF, D), FF ** -0.5, 0.109375, ((0, 32),)),
        "down_bias": normal_values(streams_of[13], (D,), 0.3, 3.0, ((0, 32),)),
    }


EPSILON = 1e-05
MASKED = -1e+30

@jax.custom_vjp
def low(v):
    return lax.optimization_barrier(v.astype(jnp.bfloat16)).astype(jnp.float32)

@jax.custom_vjp
def low_back(v):
    return v

def low_keep(v):
    return (low(v), None)

def low_pass(kept, grad):
    return (grad,)

def back_keep(v):
    return (v, None)

def back_low(kept, grad):
    return (low(grad),)
low.defvjp(low_keep, low_pass)
low_back.defvjp(back_keep, back_low)

def layer_norm(values, gain, shift):
    center = values - lax.optimization_barrier(jnp.mean(values, axis=-1, keepdims=True))
    inv_std = lax.rsqrt(lax.optimization_barrier(jnp.mean(center * center, axis=-1, keepdims=True)) + EPSILON)
    return center * inv_std * gain + shift

def tables(positions, rot_dims):
    half_dims = rot_dims // 2
    freqs = jnp.power(10000.0, -2.0 * jnp.arange(half_dims, dtype=jnp.float32) / rot_dims)
    angles = positions.astype(jnp.float32)[:, None] * freqs[None, :]
    angles = jnp.concatenate([angles, angles], axis=-1)
    return (jnp.cos(angles), jnp.sin(angles))

def turn(part, cosine, sine):
    half_dims = part.shape[-1] // 2
    swapped = jnp.concatenate([-part[..., half_dims:], part[..., :half_dims]], axis=-1)
    return part * cosine + swapped * sine

def apply_turn(packed, cosine, sine, method, rot_dims):
    paired = packed[..., :2, :]
    turned = jnp.concatenate([method(paired[..., :rot_dims], cosine, sine), paired[..., rot_dims:]], axis=-1)
    return jnp.concatenate([turned, packed[..., 2:, :]], axis=-2)

def highest_dot(left, right):
    return jnp.dot(left, right, precision=lax.Precision.HIGHEST)

def forward(row_in, params):
    gain_attn, bias_attn, gain_mlp, bias_mlp, w_qkv, b_qkv, w_proj, b_proj, w_up, b_up, w_down, b_down = params
    length = row_in.shape[0]
    in_attn = low(layer_norm(row_in, gain_attn, bias_attn))
    in_mlp = low(layer_norm(row_in, gain_mlp, bias_mlp))
    qkv_pre = low_back(highest_dot(in_attn, w_qkv) + b_qkv).reshape(length, HEADS, 3, HEAD_DIM)
    cosine, sine = tables(jnp.arange(length), ROT_DIM)
    turned = apply_turn(qkv_pre, cosine[:, None, None, :], sine[:, None, None, :], turn, ROT_DIM)
    turned = low(low_back(turned))
    queries = turned[:, :, 0, :]
    key_rows = turned[:, :, 1, :]
    value_rows = turned[:, :, 2, :]
    scale = 1.0 / math.sqrt(HEAD_DIM)
    scores = low_back(jnp.einsum('qhd,khd->hqk', queries, key_rows, precision=lax.Precision.HIGHEST) * scale)
    places = jnp.arange(length)
    allowed = places[:, None] >= places[None, :]
    scores = jnp.where(allowed[None, :, :], scores, MASKED)
    peak = lax.optimization_barrier(jnp.max(scores, axis=-1, keepdims=True))
    expo = jnp.exp(scores - peak)
    probs = low(expo / lax.optimization_barrier(jnp.sum(expo, axis=-1, keepdims=True)))
    attended = jnp.einsum('hqk,khd->qhd', probs, value_rows, precision=lax.Precision.HIGHEST)
    attended = low(low_back(attended.reshape(length, HEADS * HEAD_DIM)))
    attn_out = highest_dot(attended, w_proj) + b_proj
    up_pre = low_back(highest_dot(in_mlp, w_up) + b_up)
    activ = low(jax.nn.gelu(up_pre, approximate=False))
    mlp_out = highest_dot(activ, w_down) + b_down
    return row_in + attn_out + mlp_out

def reference(block_in, cotangent, attn_gain, attn_bias, mlp_gain, mlp_bias, qkv_weight, qkv_bias, proj_weight, proj_bias, up_weight, up_bias, down_weight, down_bias):
    params = tuple((w.astype(jnp.float32) for w in (attn_gain, attn_bias, mlp_gain, mlp_bias, qkv_weight, qkv_bias, proj_weight, proj_bias, up_weight, up_bias, down_weight, down_bias)))

    def step(totals, pair):
        row_in, row_cot = pair
        result, pull = jax.vjp(forward, row_in.astype(jnp.float32), params)
        grad_row, grad_params = pull(row_cot.astype(jnp.float32))
        totals = jax.tree.map(lambda left, right: left + right, totals, grad_params)
        return (totals, (result.astype(jnp.bfloat16), grad_row.astype(jnp.bfloat16)))
    zeros = tuple((jnp.zeros(p.shape, jnp.float32) for p in params))
    totals, (results, grads) = lax.scan(step, zeros, (block_in, cotangent))
    return (results, grads, totals[0], totals[1], totals[2], totals[3], totals[4], totals[5], totals[6], totals[7], totals[8], totals[9], totals[10], totals[11])
```

```python
import math

import jax
import jax.numpy as jnp
from jax import lax
from jax.experimental import pallas as pl
from jax.experimental.pallas import tpu as pltpu
from jax.sharding import PartitionSpec as P

HEADS = 12
HEAD_DIM = 64
ROT_DIM = 16
WIDTH = 768
EPSILON = 1e-05
MASKED = -1e30
MESH = pl.DeviceIdType.MESH
BF = jnp.bfloat16
F32 = jnp.float32
MIB = 1 << 20


def coords():
    dp = lax.axis_index("dp")
    seq = lax.axis_index("seq")
    x = lax.div(dp, 8)
    y = lax.rem(lax.div(dp, 2), 4)
    z_lo = lax.rem(dp, 2)
    z_hi = lax.div(seq, 2)
    core = lax.rem(seq, 2)
    return x, y, z_hi * 2 + z_lo, core


def device(x, y, z, core):
    return (x * 8 + y * 2 + lax.rem(z, 2), lax.div(z, 2) * 2 + core)


def around(at, offset):
    return lax.rem(at + offset, 4)


def copy_to(src, dst, send_sem, recv_sem, target):
    return pltpu.make_async_remote_copy(
        src_ref=src,
        dst_ref=dst,
        send_sem=send_sem,
        recv_sem=recv_sem,
        device_id=target,
        device_id_type=MESH,
    )


def dot(left, right):
    return jnp.dot(left, right, preferred_element_type=F32)


def dot_t(left, right):
    return lax.dot_general(left, right, (((1,), (1,)), ((), ())), preferred_element_type=F32)


def dot_a(left, right):
    return lax.dot_general(left, right, (((0,), (0,)), ((), ())), preferred_element_type=F32)


def greet(targets):
    barrier = pltpu.get_barrier_semaphore()
    for target in targets:
        pl.semaphore_signal(barrier, inc=1, device_id=target, device_id_type=MESH)
    pl.semaphore_wait(barrier, len(targets))


def weight_rows(ref):
    value = ref[...]
    return value.reshape(value.shape[0] * value.shape[1] * value.shape[2], value.shape[3])


def slab_rows(value):
    return value.reshape(value.shape[0] * value.shape[1], value.shape[2])


N_GATHER = 13


def front_kernel(
    x_in,
    g_in,
    w_a,
    w_d,
    vec_in,
    tab,
    heads,
    ob_part,
    gim_part,
    grads,
    blocks_out,
    p_other,
    xx,
    gh,
    in_attn,
    in_attn_t,
    vec,
    small,
    late,
    vecs,
    z_a,
    z_v,
    normed,
    in_mlp,
    in_mlp_t,
    send_heads,
    gg,
    pair_ss,
    pair_rs,
    one_ss,
    one_rs,
    two_ss,
    two_rs,
    head_ss,
    head_rs,
):
    x, y, z, core = coords()
    z_lo = lax.rem(z, 2)
    z_hi = lax.div(z, 2)
    x_peers = [device(around(x, o), y, z, core) for o in (1, 2, 3)]
    y_peers = [device(x, around(y, o), z, core) for o in (1, 2, 3)]
    sibling = device(x, y, z, 1 - core)
    z_pair = device(x, y, z_hi * 2 + 1 - z_lo, core)
    z_far = device(x, y, around(z, 2), core)
    greet(x_peers + y_peers + [sibling, z_pair, z_far])

    def block(i):
        return blocks_out.at[i] if i < 4 else late.at[i - 4]

    pair = [
        copy_to(w_a.at[pl.ds(0, 4)], z_a.at[pl.ds(0, 4)], pair_ss.at[0], pair_rs.at[0], z_pair),
        copy_to(vec_in, z_v, pair_ss.at[1], pair_rs.at[1], z_pair),
        copy_to(w_a.at[pl.ds(4, 4)], z_a.at[pl.ds(4, 4)], pair_ss.at[2], pair_rs.at[2], z_pair),
    ]
    for half in range(2):
        pair.append(
            copy_to(
                w_d.at[half],
                late.at[4 + half * 2 + z_lo, x, y],
                pair_ss.at[3 + half],
                pair_rs.at[3 + half],
                z_pair,
            )
        )
    for item in pair:
        item.start()
    tokens = [
        copy_to(x_in, xx.at[core], pair_ss.at[5], pair_rs.at[5], sibling),
        copy_to(g_in, gg.at[core], pair_ss.at[6], pair_rs.at[6], sibling),
    ]
    for item in tokens:
        item.start()
    xx[core] = x_in[...]
    gg[core] = g_in[...]
    for half in range(2):
        late[4 + half * 2 + z_lo, x, y] = w_d[half]

    def assemble(i):
        own = w_a[i].astype(F32)
        other = z_a[i].astype(F32)
        first = z_lo == 0
        both = jnp.concatenate(
            [jnp.where(first, own, other), jnp.where(first, other, own)], axis=0
        ).astype(BF)
        block(i)[x, y] = both

    def gather_ref(i):
        return vecs if i == 12 else block(i)

    def phase(i, number):
        ref = gather_ref(i)
        along_y = (i % 2 == 0) == (number == 1)
        ss, rs = (one_ss, one_rs) if number == 1 else (two_ss, two_rs)
        copies = []
        for k, o in enumerate((1, 2, 3)):
            target = y_peers[k] if along_y else x_peers[k]
            if number == 1:
                part = ref.at[x, y]
            elif along_y:
                part = ref.at[:, y]
            else:
                part = ref.at[x]
            copies.append(copy_to(part, part, ss.at[i, k], rs.at[i, k], target))
        return copies

    def arrivals(i, number):
        ref = gather_ref(i)
        along_y = (i % 2 == 0) == (number == 1)
        ss, rs = (one_ss, one_rs) if number == 1 else (two_ss, two_rs)
        for k, o in enumerate((1, 2, 3)):
            xs = x if along_y else around(x, 4 - o)
            ys = around(y, 4 - o) if along_y else y
            if number == 1:
                part = ref.at[xs, ys]
            elif along_y:
                part = ref.at[:, ys]
            else:
                part = ref.at[xs]
            target = y_peers[k] if along_y else x_peers[k]
            copy_to(part, part, ss.at[i, k], rs.at[i, k], target).wait_recv()

    def start(i, number):
        for item in phase(i, number):
            item.start()

    early_ids = (12, 0, 1, 2, 3)
    late_ids = tuple(range(4, 12))
    pair[0].wait_recv()
    pair[1].wait_recv()
    vecs[x, y] = (vec_in[...].astype(F32) + z_v[...].astype(F32)).astype(BF)
    for i in range(4):
        assemble(i)
    for i in early_ids:
        start(i, 1)
    pair[2].wait_recv()
    pair[3].wait_recv()
    pair[4].wait_recv()
    for i in range(4, 8):
        assemble(i)
    for item in tokens:
        item.wait_recv()

    for half in range(2):

        @pl.loop(0, 2)
        def _(step):
            rows = pl.ds(pl.multiple_of(step * 128, 128), 128)
            out_rows = pl.ds(pl.multiple_of(half * 256 + step * 128, 128), 128)
            values = xx[half, rows, :].astype(F32)
            center = values - jnp.mean(values, axis=-1, keepdims=True)
            inv_std = lax.rsqrt(jnp.mean(center * center, axis=-1, keepdims=True) + EPSILON)
            normed[out_rows, :] = center * inv_std
            cot = gg[half, rows, :]
            gh[0, out_rows, :] = cot[:, :384]
            gh[1, out_rows, :] = cot[:, 384:]

    for i in early_ids:
        arrivals(i, 1)
        start(i, 2)
    for i in late_ids:
        start(i, 1)
    arrivals(12, 2)
    total = jnp.zeros((16, WIDTH), F32)
    for i in range(4):
        for j in range(4):
            total = total + vecs[i, j].astype(F32)
    vec[...] = total

    @pl.loop(0, 4)
    def _(step):
        rows = pl.ds(pl.multiple_of(step * 128, 128), 128)
        values = normed[rows, :]
        in_attn[rows, :] = (values * vec[0:1, :] + vec[1:2, :]).astype(BF)
        in_mlp[rows, :] = (values * vec[2:3, :] + vec[3:4, :]).astype(BF)

    in_attn_t[...] = in_attn[...].T
    in_mlp_t[...] = in_mlp[...].T

    for i in (3, 0, 1, 2):
        arrivals(i, 2)
    swap_p = copy_to(blocks_out.at[3], p_other, pair_ss.at[7], pair_rs.at[7], sibling)
    swap_p.start()
    for i in late_ids:
        arrivals(i, 1)
        start(i, 2)

    cosine = tab[0]
    left_sine = tab[1]
    right_sine = tab[2]
    activations = in_attn[...]
    value_pre = dot(activations, weight_rows(blocks_out.at[2]))
    value_pre = (value_pre + vec[7:8, :384]).astype(BF)
    swap_p.wait_recv()
    for group in range(2):
        far = z_hi != group
        pre = dot(activations, weight_rows(blocks_out.at[group]))
        pre = pre + vec[6:7, group * 384 : group * 384 + 384]
        own_p = slab_rows(blocks_out[3, group * 2 + core])
        other_p = slab_rows(p_other[group * 2 + core])
        grad_att = dot_t(gh[core], own_p) + dot_t(gh[1 - core], other_p)
        grad_att = grad_att.astype(BF)
        for head in range(3):
            part = pre[:, head * 128 : head * 128 + 128]
            turned = (
                part * cosine
                + pltpu.roll(part, 120, 1) * left_sine
                + pltpu.roll(part, 8, 1) * right_sine
            ).astype(BF)
            at = head * 64
            rest = jnp.concatenate(
                [
                    value_pre[:, group * 192 + at : group * 192 + at + 64],
                    grad_att[:, at : at + 64],
                ],
                axis=1,
            )

            @pl.when(far)
            def _():
                send_heads[head, :, 0:128] = turned
                send_heads[head, :, 128:256] = rest

            @pl.when(jnp.logical_not(far))
            def _():
                heads[head, group, :, 0:128] = turned
                heads[head, group, :, 128:256] = rest

    far_copies = [
        copy_to(
            send_heads.at[head], heads.at[head, z_hi], head_ss.at[head], head_rs.at[head], z_far
        )
        for head in range(3)
    ]
    for item in far_copies:
        item.start()

    for i in late_ids:
        arrivals(i, 2)
    ob_part[...] = jnp.zeros((512, WIDTH), F32)
    gim_part[...] = jnp.zeros((512, WIDTH), F32)
    small[...] = jnp.zeros((16, WIDTH), F32)

    @pl.loop(0, 4)
    def _(b):
        weight_up = weight_rows(late.at[b])
        down = [
            jnp.concatenate(
                [slab_rows(late[4 + 2 * half, b]), slab_rows(late[5 + 2 * half, b])], axis=0
            )
            for half in range(2)
        ]
        bias = jnp.where(
            lax.rem(b, 2) == 0,
            jnp.where(b < 2, vec[8:9, :384], vec[9:10, :384]),
            jnp.where(b < 2, vec[8:9, 384:], vec[9:10, 384:]),
        )
        up_pre = dot(in_mlp[...], weight_up) + bias
        cdf = 0.5 * (1.0 + lax.erf(up_pre * (1.0 / math.sqrt(2.0))))
        activ = (up_pre * cdf).astype(BF)
        density = jnp.exp(-0.5 * up_pre * up_pre) * (1.0 / math.sqrt(2.0 * math.pi))
        slope = cdf + up_pre * density
        grad_activ = dot_t(gh[0], down[0]) + dot_t(gh[1], down[1])
        grad_up = grad_activ * slope
        low_grad = grad_up.astype(BF)
        bias_grad = jnp.sum(low_grad.astype(F32), axis=0, keepdims=True)
        for k in range(4):

            @pl.when(b == k)
            def _():
                small[7 + k // 2 : 8 + k // 2, (k % 2) * 384 : (k % 2) * 384 + 384] = bias_grad

        activ_t = activ.T
        for half in range(2):
            ob_part[:, half * 384 : half * 384 + 384] += dot(activ, down[half])
            grad_down = dot(activ_t, gh[half]).astype(BF)
            grads[4 + 2 * half, b] = grad_down[:192].reshape(4, 48, 384)
            grads[5 + 2 * half, b] = grad_down[192:].reshape(4, 48, 384)
        grads[b] = dot(in_mlp_t[...], low_grad).astype(BF).reshape(4, 4, 48, 384)
        gim_part[...] += dot_t(low_grad, weight_up)

    grad_in = gim_part[...]
    small[2:3, :] = jnp.sum(grad_in * normed[...], axis=0, keepdims=True)
    small[3:4, :] = jnp.sum(grad_in, axis=0, keepdims=True)
    small[4:5, :] = jnp.sum(g_in[...].astype(F32), axis=0, keepdims=True)

    for item in far_copies:
        item.wait()
    swap_p.wait_send()
    for item in pair + tokens:
        item.wait_send()
    for i in early_ids + late_ids:
        for number in (1, 2):
            for item in phase(i, number):
                item.wait_send()


def front(x_in, g_in, w_a, w_d, vec_in, tab):
    shape = jax.ShapeDtypeStruct
    outs = (
        shape((3, 2, 512, 256), BF),
        shape((512, WIDTH), F32),
        shape((512, WIDTH), F32),
        shape((8, 4, 4, 48, 384), BF),
        shape((4, 4, 4, 48, 384), BF),
        shape((4, 4, 48, 384), BF),
        shape((2, 256, WIDTH), BF),
        shape((2, 512, 384), BF),
        shape((512, WIDTH), BF),
        shape((WIDTH, 512), BF),
        shape((16, WIDTH), F32),
        shape((16, WIDTH), F32),
    )
    dma = pltpu.SemaphoreType.DMA
    vmem = pl.BlockSpec(memory_space=pltpu.VMEM)
    return pl.pallas_call(
        front_kernel,
        name="front",
        out_shape=outs,
        in_specs=[vmem] * 6,
        out_specs=(vmem,) * len(outs),
        scratch_shapes=[
            pltpu.VMEM((8, 4, 4, 48, 384), BF),
            pltpu.VMEM((4, 4, 16, WIDTH), BF),
            pltpu.VMEM((8, 24, 384), BF),
            pltpu.VMEM((16, WIDTH), BF),
            pltpu.VMEM((512, WIDTH), F32),
            pltpu.VMEM((512, WIDTH), BF),
            pltpu.VMEM((WIDTH, 512), BF),
            pltpu.VMEM((3, 512, 256), BF),
            pltpu.VMEM((2, 256, WIDTH), BF),
            dma((8,)),
            dma((8,)),
            dma((N_GATHER, 3)),
            dma((N_GATHER, 3)),
            dma((N_GATHER, 3)),
            dma((N_GATHER, 3)),
            dma((3,)),
            dma((3,)),
        ],
        compiler_params=pltpu.CompilerParams(
            collective_id=0, has_side_effects=True, vmem_limit_bytes=60 * MIB
        ),
    )(x_in, g_in, w_a, w_d, vec_in, tab)


def back_kernel(
    heads,
    ob_part,
    gim_part,
    mlp_grads,
    weights,
    p_other,
    xx,
    gh,
    in_attn,
    in_attn_t,
    vec,
    small_in,
    tab,
    g_in,
    block_out,
    input_grad,
    owned,
    owned_down,
    small,
    attn_grads,
    own_rows,
    far_rows,
    back_rows,
    dk_acc,
    dv_acc,
    att,
    att_other,
    grad_qk,
    grad_v,
    h_part,
    token_in,
    r_one,
    mid,
    r_two,
    done,
    r_z,
    share,
    small_r,
    one_ss,
    one_rs,
    two_ss,
    two_rs,
    z_ss,
    z_rs,
    head_ss,
    head_rs,
    pair_ss,
    pair_rs,
    small_ss,
    small_rs,
    share_ss,
    share_rs,
):
    x, y, z, core = coords()
    z_lo = lax.rem(z, 2)
    z_hi = lax.div(z, 2)
    x_peers = [device(around(x, o), y, z, core) for o in (1, 2, 3)]
    y_peers = [device(x, around(y, o), z, core) for o in (1, 2, 3)]
    z_peers = [device(x, y, around(z, o), core) for o in (1, 2, 3)]
    z_cross = [device(x, y, around(z, o), 1 - core) for o in (1, 2, 3)]
    sibling = device(x, y, z, 1 - core)
    z_far = z_peers[1]
    greet(x_peers + y_peers + z_peers + z_cross + [sibling])

    def grad_ref(i):
        return attn_grads.at[i] if i < 4 else mlp_grads.at[i - 4]

    def first_copies(i):
        ref = grad_ref(i)
        copies = []
        for k, o in enumerate((1, 2, 3)):
            if i % 2 == 0:
                part, target = ref.at[around(x, o)], x_peers[k]
            else:
                part, target = ref.at[:, around(y, o)], y_peers[k]
            copies.append(copy_to(part, r_one.at[i, k], one_ss.at[i, k], one_rs.at[i, k], target))
        return copies

    def second_copies(i):
        copies = []
        for k, o in enumerate((1, 2, 3)):
            if i % 2 == 0:
                part, target = mid.at[i, around(y, o)], y_peers[k]
            else:
                part, target = mid.at[i, around(x, o)], x_peers[k]
            copies.append(copy_to(part, r_two.at[i, k], two_ss.at[i, k], two_rs.at[i, k], target))
        return copies

    def third_copies(group):
        return [
            copy_to(
                done.at[group * 4 + around(z, o)],
                r_z.at[group, k],
                z_ss.at[group, k],
                z_rs.at[group, k],
                z_peers[k],
            )
            for k, o in enumerate((1, 2, 3))
        ]

    def first_sum(i):
        for item in first_copies(i):
            item.wait_recv()
        ref = grad_ref(i)

        @pl.loop(0, 4)
        def _(j):
            own = ref[x, j] if i % 2 == 0 else ref[j, y]
            total = own.astype(F32)
            for k in range(3):
                total = total + r_one[i, k, j].astype(F32)
            mid[i, j] = total.astype(BF)

    def second_sum(i):
        for item in second_copies(i):
            item.wait_recv()
        total = mid[i, y if i % 2 == 0 else x].astype(F32)
        for k in range(3):
            total = total + r_two[i, k].astype(F32)
        done[i] = total.astype(BF)

    def third_sum(group):
        for item in third_copies(group):
            item.wait_recv()
        total = done[group * 4 + z].astype(F32)
        for k in range(3):
            total = total + r_z[group, k].astype(F32)
        return total

    def start(copies):
        for item in copies:
            item.start()

    mlp_ids = tuple(range(4, 12))
    attn_ids = tuple(range(4))
    for i in mlp_ids:
        start(first_copies(i))

    scale = 1.0 / math.sqrt(HEAD_DIM)

    def far_copy(head):
        return copy_to(
            far_rows.at[head],
            back_rows.at[head],
            head_ss.at[head],
            head_rs.at[head],
            z_far,
        )

    @pl.loop(0, 3)
    def _(head):
        packed = heads[head].reshape(1024, 256)
        queries = packed[:, 0:64]
        key_rows = packed[:, 64:128]
        value_rows = packed[:, 128:192]
        grad_rows = packed[:, 192:256]
        dk_acc[...] = jnp.zeros((1024, HEAD_DIM), F32)
        dv_acc[...] = jnp.zeros((1024, HEAD_DIM), F32)
        dq_parts = []
        out_parts = []
        for blk in range(4):
            lo, hi = blk * 256, blk * 256 + 256
            q = queries[lo:hi]
            do = grad_rows[lo:hi]
            scores = dot_t(q, key_rows[:hi]) * scale
            row_place = lax.broadcasted_iota(jnp.int32, (256, hi), 0) + lo
            col_place = lax.broadcasted_iota(jnp.int32, (256, hi), 1)
            scores = jnp.where(row_place >= col_place, scores, MASKED)
            peak = jnp.max(scores, axis=-1, keepdims=True)
            expo = jnp.exp(scores - peak)
            probs = expo * (1.0 / jnp.sum(expo, axis=-1, keepdims=True))
            low_probs = probs.astype(BF)
            out_parts.append(dot(low_probs, value_rows[:hi]).astype(BF))
            grad_probs = dot_t(do, value_rows[:hi])
            inner = jnp.sum(probs * grad_probs, axis=-1, keepdims=True)
            grad_scores = (probs * (grad_probs - inner)).astype(BF)
            dq_parts.append((dot(grad_scores, key_rows[:hi]) * scale).astype(BF))
            dk_acc[:hi, :] += dot_a(grad_scores, q)
            dv_acc[:hi, :] += dot_a(low_probs, do)
        dk = (dk_acc[...] * scale).astype(BF)
        dv = dv_acc[...].astype(BF)
        dq = jnp.concatenate(dq_parts, axis=0)
        out = jnp.concatenate(out_parts, axis=0)
        result = jnp.concatenate([dq, dk, dv, out], axis=1)
        near = z_hi == 0
        own_rows[head] = jnp.where(near, result[:512], result[512:])
        far_rows[head] = jnp.where(near, result[512:], result[:512])
        far_copy(head).start()

    for i in mlp_ids:
        first_sum(i)
        start(second_copies(i))
    for i in mlp_ids:
        second_sum(i)
    start(third_copies(1))
    start(third_copies(2))

    for head in range(3):
        far_copy(head).wait_recv()
    cosine = tab[0]
    left_sine = tab[1]
    right_sine = tab[2]
    for group in range(2):
        mine = z_hi == group
        for head in range(3):
            rows = jnp.where(mine, own_rows[head], back_rows[head])
            part = rows[:, 0:128].astype(F32)
            turned = (
                part * cosine
                - pltpu.roll(part, 120, 1) * left_sine
                - pltpu.roll(part, 8, 1) * right_sine
            ).astype(BF)
            grad_qk[group, :, head * 128 : head * 128 + 128] = turned
            grad_v[:, group * 192 + head * 64 : group * 192 + head * 64 + 64] = rows[:, 128:192]
            att[group, :, head * 64 : head * 64 + 64] = rows[:, 192:256]
    swap_att = copy_to(att, att_other, pair_ss.at[0], pair_rs.at[0], sibling)
    swap_att.start()

    for group in range(2):
        attn_grads[group] = dot(in_attn_t[...], grad_qk[group]).astype(BF).reshape(4, 4, 48, 384)
        start(first_copies(group))
    attn_grads[2] = dot(in_attn_t[...], grad_v[...]).astype(BF).reshape(4, 4, 48, 384)
    start(first_copies(2))
    swap_att.wait_recv()
    for group in range(2):
        attn_grads[3, group * 2 + core] = (
            dot_a(att[group], gh[core]).astype(BF).reshape(4, 48, 384)
        )
        attn_grads[3, group * 2 + 1 - core] = (
            dot_a(att_other[group], gh[core]).astype(BF).reshape(4, 48, 384)
        )
    start(first_copies(3))

    small[...] = small_in[...]
    for group in range(2):
        small[5:6, group * 384 : group * 384 + 384] = jnp.sum(
            grad_qk[group].astype(F32), axis=0, keepdims=True
        )
    small[6:7, :384] = jnp.sum(grad_v[...].astype(F32), axis=0, keepdims=True)
    grad_in = (
        dot_t(grad_qk[0], weight_rows(weights.at[0]))
        + dot_t(grad_qk[1], weight_rows(weights.at[1]))
        + dot_t(grad_v[...], weight_rows(weights.at[2]))
    )
    h_part[...] = grad_in * vec[0:1, :] + gim_part[...] * vec[2:3, :]
    small[1:2, :] = jnp.sum(grad_in, axis=0, keepdims=True)
    gain_grad = jnp.zeros((1, WIDTH), F32)
    for half in range(2):
        values = xx[half].astype(F32)
        center = values - jnp.mean(values, axis=-1, keepdims=True)
        inv_std = lax.rsqrt(jnp.mean(center * center, axis=-1, keepdims=True) + EPSILON)
        gain_grad = gain_grad + jnp.sum(
            grad_in[half * 256 : half * 256 + 256] * (center * inv_std), axis=0, keepdims=True
        )
    small[0:1, :] = gain_grad

    def small_copies(number):
        peers = (x_peers, y_peers, z_peers)[number]
        return [
            copy_to(
                small_r.at[9 + number],
                small_r.at[number * 3 + k],
                small_ss.at[number, k],
                small_rs.at[number, k],
                peers[k],
            )
            for k in range(3)
        ]

    def small_sum(number):
        total = small_r[9 + number]
        for k, item in enumerate(small_copies(number)):
            item.wait_recv()
            total = total + small_r[number * 3 + k]
        return total

    small_r[9] = small[...]
    start(small_copies(0))

    other_rows = pl.ds(pl.multiple_of((1 - core) * 256, 256), 256)
    my_rows = pl.ds(pl.multiple_of(core * 256, 256), 256)
    swap_h = copy_to(
        h_part.at[other_rows], token_in.at[0], pair_ss.at[1], pair_rs.at[1], sibling
    )
    swap_h.start()
    for group in range(2):
        own_p = slab_rows(weights[3, group * 2 + core])
        other_p = slab_rows(p_other[group * 2 + core])
        left = att[group]
        for half in range(2):
            cols = slice(half * 384, half * 384 + 384)
            matrix = jnp.where(core == half, own_p, other_p)
            ob_part[:, cols] += dot(left, matrix)
    swap_ob = copy_to(
        ob_part.at[other_rows], token_in.at[1], pair_ss.at[2], pair_rs.at[2], sibling
    )
    swap_ob.start()

    for i in attn_ids:
        first_sum(i)
        start(second_copies(i))
    small_r[10] = small_sum(0)
    start(small_copies(1))

    swap_h.wait_recv()
    swap_ob.wait_recv()
    values = xx[core].astype(F32)
    center = values - jnp.mean(values, axis=-1, keepdims=True)
    inv_std = lax.rsqrt(jnp.mean(center * center, axis=-1, keepdims=True) + EPSILON)
    norm_rows = center * inv_std
    grad_norm = h_part[my_rows, :] + token_in[0]
    input_grad[...] = (
        g_in[...].astype(F32)
        + inv_std
        * (
            grad_norm
            - jnp.mean(grad_norm, axis=-1, keepdims=True)
            - norm_rows * jnp.mean(grad_norm * norm_rows, axis=-1, keepdims=True)
        )
    ).astype(BF)
    block_out[...] = (
        values + ob_part[my_rows, :] + token_in[1] + (vec[4:5, :] + vec[5:6, :])
    ).astype(BF)

    for i in attn_ids:
        second_sum(i)
    start(third_copies(0))
    small_r[11] = small_sum(1)
    start(small_copies(2))

    def split_rows(group, total):
        share[0, group] = total[:24].astype(BF)
        share[1, group] = total[24:].astype(BF)

    split_rows(1, third_sum(1))
    down_total = third_sum(2).astype(BF)
    owned_down[core, z_hi] = down_total
    split_rows(0, third_sum(0))
    owned[core, z] = share[z_lo]

    peers = []
    for k, o in enumerate((1, 2, 3)):
        peers.append((z_peers[k], around(z, o), around(z, 4 - o), core, k))
        peers.append((z_cross[k], around(z, o), around(z, 4 - o), 1 - core, 3 + k))
    peers.append((sibling, z, z, 1 - core, 6))
    share_copies = []
    share_waits = []
    for target, z_to, z_from, core_from, k in peers:
        share_copies.append(
            copy_to(
                share.at[lax.rem(z_to, 2)],
                owned.at[core, z],
                share_ss.at[k],
                share_rs.at[k],
                target,
            )
        )
        share_waits.append(
            copy_to(
                share.at[0],
                owned.at[core_from, z_from],
                share_ss.at[k],
                share_rs.at[k],
                target,
            )
        )
    for target, core_from, hi_from, k in (
        (z_peers[1], core, 1 - z_hi, 7),
        (z_cross[1], 1 - core, 1 - z_hi, 8),
        (sibling, 1 - core, z_hi, 9),
    ):
        share_copies.append(
            copy_to(
                owned_down.at[core, z_hi],
                owned_down.at[core, z_hi],
                share_ss.at[k],
                share_rs.at[k],
                target,
            )
        )
        share_waits.append(
            copy_to(
                owned_down.at[core_from, hi_from],
                owned_down.at[core_from, hi_from],
                share_ss.at[k],
                share_rs.at[k],
                target,
            )
        )
    start(share_copies)
    small_r[12] = small_sum(2)
    swap_small = copy_to(
        small_r.at[12], small_r.at[13], pair_ss.at[3], pair_rs.at[3], sibling
    )
    swap_small.start()
    swap_small.wait_recv()
    small[...] = jnp.zeros((16, WIDTH), F32)
    small[0:8, :] = small_r[12, 0:8, :] + small_r[13, 0:8, :]
    for row in range(4):
        low = jnp.where(core == 0, small_r[12, 5 + row : 6 + row, :], small_r[13, 5 + row : 6 + row, :])
        high = jnp.where(core == 0, small_r[13, 5 + row : 6 + row, :], small_r[12, 5 + row : 6 + row, :])
        small[5 + row : 6 + row, :] = low
        small[9 + row : 10 + row, :] = high

    for item in share_waits:
        item.wait_recv()
    for item in share_copies + [swap_att, swap_h, swap_ob, swap_small]:
        item.wait_send()
    for head in range(3):
        far_copy(head).wait_send()
    for i in attn_ids + mlp_ids:
        for item in first_copies(i) + second_copies(i):
            item.wait_send()
    for group in range(3):
        for item in third_copies(group):
            item.wait_send()
    for number in range(3):
        for item in small_copies(number):
            item.wait_send()


def back(heads, ob_part, gim_part, mlp_grads, weights, p_other, xx, gh, in_attn, in_attn_t, vec, small_in, tab, g_in):
    shape = jax.ShapeDtypeStruct
    outs = (
        shape((256, WIDTH), BF),
        shape((256, WIDTH), BF),
        shape((2, 4, 2, 24, 384), BF),
        shape((2, 2, 48, 384), BF),
        shape((16, WIDTH), F32),
    )
    dma = pltpu.SemaphoreType.DMA
    vmem = pl.BlockSpec(memory_space=pltpu.VMEM)
    return pl.pallas_call(
        back_kernel,
        name="back",
        out_shape=outs,
        in_specs=[vmem] * 14,
        out_specs=(vmem,) * len(outs),
        scratch_shapes=[
            pltpu.VMEM((4, 4, 4, 48, 384), BF),
            pltpu.VMEM((3, 512, 256), BF),
            pltpu.VMEM((3, 512, 256), BF),
            pltpu.VMEM((3, 512, 256), BF),
            pltpu.VMEM((1024, HEAD_DIM), F32),
            pltpu.VMEM((1024, HEAD_DIM), F32),
            pltpu.VMEM((2, 512, 192), BF),
            pltpu.VMEM((2, 512, 192), BF),
            pltpu.VMEM((2, 512, 384), BF),
            pltpu.VMEM((512, 384), BF),
            pltpu.VMEM((512, WIDTH), F32),
            pltpu.VMEM((2, 256, WIDTH), F32),
            pltpu.VMEM((12, 3, 4, 48, 384), BF),
            pltpu.VMEM((12, 4, 48, 384), BF),
            pltpu.VMEM((12, 3, 48, 384), BF),
            pltpu.VMEM((12, 48, 384), BF),
            pltpu.VMEM((3, 3, 48, 384), BF),
            pltpu.VMEM((2, 2, 24, 384), BF),
            pltpu.VMEM((14, 16, WIDTH), F32),
            dma((12, 3)),
            dma((12, 3)),
            dma((12, 3)),
            dma((12, 3)),
            dma((3, 3)),
            dma((3, 3)),
            dma((3,)),
            dma((3,)),
            dma((4,)),
            dma((4,)),
            dma((3, 3)),
            dma((3, 3)),
            dma((10,)),
            dma((10,)),
        ],
        compiler_params=pltpu.CompilerParams(
            collective_id=1, has_side_effects=True, vmem_limit_bytes=60 * MIB
        ),
    )(heads, ob_part, gim_part, mlp_grads, weights, p_other, xx, gh, in_attn, in_attn_t, vec, small_in, tab, g_in)


def rotary_tables(first, count):
    half = ROT_DIM // 2
    freqs = jnp.power(10000.0, -2.0 * jnp.arange(half, dtype=F32) / ROT_DIM)
    angles = (first + jnp.arange(count)).astype(F32)[:, None] * freqs[None, :]
    cosine, sine = jnp.cos(angles), jnp.sin(angles)
    ones = jnp.ones((count, HEAD_DIM - ROT_DIM), F32)
    zero_half = jnp.zeros((count, half), F32)
    cos_row = jnp.concatenate([cosine, cosine, ones], axis=1)
    left = jnp.concatenate([-sine, zero_half, ones * 0.0], axis=1)
    right = jnp.concatenate([zero_half, sine, ones * 0.0], axis=1)
    return jnp.stack([jnp.tile(t, (1, 2)) for t in (cos_row, left, right)])


def place(values, owner, count):
    each = values.shape[0]
    spots = jnp.arange(count) // each
    return jnp.where(spots == owner, jnp.tile(values, count // each), jnp.zeros((), values.dtype))


def local(
    block_in,
    cotangent,
    attn_gain,
    attn_bias,
    mlp_gain,
    mlp_bias,
    qkv_weight,
    qkv_bias,
    proj_weight,
    proj_bias,
    up_weight,
    up_bias,
    down_weight,
    down_bias,
):
    dp = lax.axis_index("dp")
    seq = lax.axis_index("seq")
    core = seq % 2

    def mine(array, axis):
        return lax.dynamic_index_in_dim(array, core, axis, keepdims=False)

    qkv = mine(qkv_weight.reshape(24, 2, 2, 3, 3, HEAD_DIM), 2)
    w_qk = qkv[:, :, :, :2, :].reshape(24, 2, 384).transpose(1, 0, 2)
    w_v = qkv[:, :, :, 2, :].reshape(1, 24, 384)
    w_p = mine(proj_weight.reshape(24, 2, 384), 1)[None]
    w_u = mine(up_weight.reshape(24, 4, 4, 2, 2, 48), 4)
    w_u = w_u.transpose(1, 0, 3, 2, 4).reshape(4, 24, 384)
    w_a = jnp.concatenate([w_qk, w_v, w_p, w_u], axis=0)
    w_d = mine(down_weight.reshape(2, 48, 2, 384), 0).transpose(1, 0, 2)

    b_qkv = mine(place(qkv_bias, dp, 2304).reshape(2, 2, 3, 3, HEAD_DIM), 1)
    b_qk = b_qkv[:, :, :2, :].reshape(768)
    b_v = b_qkv[:, :, 2, :].reshape(384)
    b_u = mine(place(up_bias, dp, 3072).reshape(4, 4, 2, 2, 48), 3)
    b_u = b_u.transpose(0, 2, 1, 3).reshape(2, 768)
    rows = [place(v, dp, 768) for v in (attn_gain, attn_bias, mlp_gain, mlp_bias, proj_bias, down_bias)]
    rows += [b_qk, jnp.concatenate([b_v, jnp.zeros((384,), BF)]), b_u[0], b_u[1]]
    rows += [jnp.zeros((768,), BF)] * 6
    vec_in = jnp.stack(rows)

    tab = rotary_tables((seq // 2) * 512, 512)
    x_in = block_in.reshape(256, WIDTH)
    g_in = cotangent.reshape(256, WIDTH)
    (heads, ob_part, gim_part, mlp_grads, weights, p_other, xx, gh, in_attn, in_attn_t, vec, small) = front(
        x_in, g_in, w_a, w_d, vec_in, tab
    )
    block_out, input_grad, owned, owned_down, small = back(
        heads, ob_part, gim_part, mlp_grads, weights, p_other, xx, gh, in_attn, in_attn_t, vec, small, tab, g_in
    )

    owned = owned.astype(F32)
    g_qk = owned[:, 0:2, 0].reshape(2, 2, 24, 3, 2, HEAD_DIM)
    g_v = owned[:, 2, 0].reshape(2, 24, 2, 3, 1, HEAD_DIM).transpose(0, 2, 1, 3, 4, 5)
    g_qkv = jnp.concatenate([g_qk, g_v], axis=4)
    g_qkv = g_qkv.transpose(2, 1, 0, 3, 4, 5).reshape(24, 2304)
    g_proj = owned[:, 3, 0].transpose(1, 0, 2).reshape(24, 768)
    g_up = owned[:, :, 1].reshape(2, 4, 24, 2, 4, 48)
    g_up = g_up.transpose(2, 1, 4, 3, 0, 5).reshape(24, 3072)
    g_down = owned_down.astype(F32).transpose(0, 2, 1, 3).reshape(96, 768)

    def part(row, each):
        return lax.dynamic_slice_in_dim(row, dp * each, each)

    bias_qk = jnp.stack([small[5], small[9]]).reshape(2, 2, 3, 2, HEAD_DIM)
    bias_v = jnp.stack([small[6, :384], small[10, :384]]).reshape(2, 2, 3, 1, HEAD_DIM)
    bias_qkv = jnp.concatenate([bias_qk, bias_v], axis=3).transpose(1, 0, 2, 3, 4).reshape(2304)
    bias_up = jnp.stack([small[7:9].reshape(1536), small[11:13].reshape(1536)])
    bias_up = bias_up.reshape(2, 4, 2, 4, 48).transpose(1, 3, 2, 0, 4).reshape(3072)
    out_total = part(small[4], 24)
    return (
        block_out.reshape(1, 256, WIDTH),
        input_grad.reshape(1, 256, WIDTH),
        part(small[0], 24),
        part(small[1], 24),
        part(small[2], 24),
        part(small[3], 24),
        g_qkv,
        part(bias_qkv, 72),
        g_proj,
        out_total,
        g_up,
        part(bias_up, 96),
        g_down,
        out_total,
    )


def solution(mesh):
    tokens = P("dp", "seq", None)
    in_specs = (tokens, tokens) + (P("dp"),) * 4 + (P("dp", None), P("dp")) * 4
    return jax.shard_map(
        local, mesh=mesh, in_specs=in_specs, out_specs=in_specs, check_vma=False
    )
```

```python
import math

import jax
import jax.numpy as jnp
import numpy as np
from jax import lax
from jax.experimental import pallas as pl
from jax.experimental.pallas import tpu as pltpu
from jax.sharding import PartitionSpec as P

HEADS = 12
HEAD_DIM = 64
ROT_DIM = 16
WIDTH = 768
EPSILON = 1e-05
MASKED = -1e30
MESH = pl.DeviceIdType.MESH
BF = jnp.bfloat16
F32 = jnp.float32
MIB = 1 << 20


def coords():
    dp = lax.axis_index("dp")
    seq = lax.axis_index("seq")
    x = lax.div(dp, 8)
    y = lax.rem(lax.div(dp, 2), 4)
    z_lo = lax.rem(dp, 2)
    z_hi = lax.div(seq, 2)
    core = lax.rem(seq, 2)
    return x, y, z_hi * 2 + z_lo, core


def device(x, y, z, core):
    return (x * 8 + y * 2 + lax.rem(z, 2), lax.div(z, 2) * 2 + core)


def around(at, offset):
    return lax.rem(at + offset, 4)


def copy_to(src, dst, send_sem, recv_sem, target):
    return pltpu.make_async_remote_copy(
        src_ref=src,
        dst_ref=dst,
        send_sem=send_sem,
        recv_sem=recv_sem,
        device_id=target,
        device_id_type=MESH,
    )


def dot(left, right):
    return jnp.dot(left, right, preferred_element_type=F32)


def dot_t(left, right):
    return lax.dot_general(left, right, (((1,), (1,)), ((), ())), preferred_element_type=F32)


def dot_a(left, right):
    return lax.dot_general(left, right, (((0,), (0,)), ((), ())), preferred_element_type=F32)


def greet(targets):
    barrier = pltpu.get_barrier_semaphore()
    for target in targets:
        pl.semaphore_signal(barrier, inc=1, device_id=target, device_id_type=MESH)
    pl.semaphore_wait(barrier, len(targets))


def weight_rows(ref):
    value = ref[...]
    return value.reshape(value.shape[0] * value.shape[1] * value.shape[2], value.shape[3])


def slab_rows(value):
    return value.reshape(value.shape[0] * value.shape[1], value.shape[2])


N_BLOCK = 6
QK, VP = 4, 5


def whole_kernel(
    x_in,
    g_in,
    w_a,
    vec_in,
    tab,
    block_out,
    input_grad,
    owned,
    small,
    weights,
    vecs,
    z_a,
    z_v,
    vec,
    xx,
    gg,
    normed,
    in_attn,
    in_attn_t,
    in_mlp,
    in_mlp_t,
    activ,
    low_grad,
    ob_part,
    gim_part,
    grads,
    p_send,
    p_recv,
    p_rows,
    qk_rows,
    vd_rows,
    dk_acc,
    dv_acc,
    att,
    grad_qk,
    grad_v,
    pg_send,
    pg_recv,
    r_one,
    mid,
    r_two,
    kept,
    z_send,
    z_recv,
    sums,
    swap_f,
    swap_r,
    far_b,
    far_r,
    small_b,
    small_r,
    pair_ss,
    pair_rs,
    tok_ss,
    tok_rs,
    one_ss,
    one_rs,
    two_ss,
    two_rs,
    p_ss,
    p_rs,
    sone_ss,
    sone_rs,
    stwo_ss,
    stwo_rs,
    z_ss,
    z_rs,
    share_ss,
    share_rs,
    swap_ss,
    swap_rs,
    small_ss,
    small_rs,
):
    x, y, z, core = coords()
    z_lo = lax.rem(z, 2)
    z_hi = lax.div(z, 2)
    me = z_hi * 2 + core
    x_peers = [device(around(x, o), y, z, core) for o in (1, 2, 3)]
    y_peers = [device(x, around(y, o), z, core) for o in (1, 2, 3)]
    z_far = around(z, 2)
    sibling = device(x, y, z, 1 - core)
    far = device(x, y, z_far, core)
    cross = device(x, y, z_far, 1 - core)
    z_pair = device(x, y, z_hi * 2 + 1 - z_lo, core)
    group = [sibling, far, cross]
    group_ids = [z_hi * 2 + 1 - core, (1 - z_hi) * 2 + core, (1 - z_hi) * 2 + 1 - core]
    greet(x_peers + y_peers + group + [z_pair])

    def token_rows(index):
        return pl.ds(pl.multiple_of(index * 256, 256), 256)

    def start(copies):
        for item in copies:
            item.start()

    pair = [copy_to(vec_in, z_v, pair_ss.at[0], pair_rs.at[0], z_pair)]
    for k in range(3):
        part = pl.ds(2 * k, 2)
        pair.append(
            copy_to(w_a.at[part], z_a.at[part], pair_ss.at[1 + k], pair_rs.at[1 + k], z_pair)
        )
    start([pair[1], pair[0], pair[2], pair[3]])

    mine = token_rows(me)
    theirs = token_rows(group_ids[1])
    tokens = []
    for k, (source, held) in enumerate(((x_in, xx), (g_in, gg))):
        tokens.append(
            (
                copy_to(source, held.at[mine], tok_ss.at[k, 0], tok_rs.at[k, 0], sibling),
                copy_to(source, held.at[mine], tok_ss.at[k, 1], tok_rs.at[k, 1], far),
                copy_to(held.at[theirs], held.at[theirs], tok_ss.at[k, 2], tok_rs.at[k, 2], sibling),
            )
        )
    for k in range(2):
        tokens[k][1].start()
        tokens[k][0].start()
    xx[mine, :] = x_in[...]
    gg[mine, :] = g_in[...]

    def assemble(i):
        own = w_a[i].astype(F32)
        other = z_a[i].astype(F32)
        first = z_lo == 0
        weights[i, x, y] = jnp.concatenate(
            [jnp.where(first, own, other), jnp.where(first, other, own)], axis=0
        ).astype(BF)

    def gather_ref(i):
        return vecs if i == N_BLOCK else weights.at[i]

    def gather(i, number, arriving=False):
        ref = gather_ref(i)
        along_y = (i % 2 == 0) == (number == 1)
        ss, rs = (one_ss, one_rs) if number == 1 else (two_ss, two_rs)
        copies = []
        for k, o in enumerate((1, 2, 3)):
            target = y_peers[k] if along_y else x_peers[k]
            xs, ys = x, y
            if arriving and along_y:
                ys = around(y, 4 - o)
            elif arriving:
                xs = around(x, 4 - o)
            if number == 1:
                part = ref.at[xs, ys]
            elif along_y:
                part = ref.at[:, ys]
            else:
                part = ref.at[xs]
            copies.append(copy_to(part, part, ss.at[i, k], rs.at[i, k], target))
        return copies

    def arrived(i, number):
        for item in gather(i, number, True):
            item.wait_recv()

    def layer_norm(index):
        for step in range(2):
            rows = pl.ds(pl.multiple_of(index * 256 + step * 128, 128), 128)
            values = xx[rows, :].astype(F32)
            center = values - jnp.mean(values, axis=-1, keepdims=True)
            inv_std = lax.rsqrt(jnp.mean(center * center, axis=-1, keepdims=True) + EPSILON)
            normed[rows, :] = center * inv_std

    pair[1].wait_recv()
    assemble(0)
    assemble(1)
    start(gather(0, 1) + gather(1, 1))
    pair[0].wait_recv()
    vecs[x, y] = (vec_in[...].astype(F32) + z_v[...].astype(F32)).astype(BF)
    start(gather(N_BLOCK, 1))
    pair[2].wait_recv()
    assemble(2)
    assemble(3)
    start(gather(2, 1) + gather(3, 1))
    pair[3].wait_recv()
    assemble(4)
    assemble(5)
    start(gather(4, 1) + gather(5, 1))
    layer_norm(me)
    for i in (0, 1, N_BLOCK, 2, 3, 4, 5):
        arrived(i, 1)
        start(gather(i, 2))
    tokens[0][0].wait_recv()
    layer_norm(group_ids[0])
    tokens[0][1].wait_recv()
    tokens[0][2].start()
    layer_norm(group_ids[1])
    tokens[0][2].wait_recv()
    layer_norm(group_ids[2])
    arrived(N_BLOCK, 2)
    total = jnp.zeros((16, WIDTH), F32)
    for i in range(4):
        for j in range(4):
            total = total + vecs[i, j].astype(F32)
    vec[...] = total

    @pl.loop(0, 4)
    def _(step):
        rows = token_rows(step)
        values = normed[rows, :]
        attn_rows = (values * vec[0:1, :] + vec[1:2, :]).astype(BF)
        mlp_rows = (values * vec[2:3, :] + vec[3:4, :]).astype(BF)
        in_attn[rows, :] = attn_rows
        in_mlp[rows, :] = mlp_rows
        in_attn_t[:, rows] = attn_rows.T
        in_mlp_t[:, rows] = mlp_rows.T

    tokens[1][1].wait_recv()
    tokens[1][2].start()
    tokens[1][0].wait_recv()
    arrived(0, 2)
    arrived(1, 2)
    arrived(2, 2)
    arrived(3, 2)
    tokens[1][2].wait_recv()

    def first_copies(i):
        ref = grads.at[i]
        copies = []
        for k, o in enumerate((1, 2, 3)):
            if i % 2 == 0:
                part, target = ref.at[around(x, o)], x_peers[k]
            else:
                part, target = ref.at[:, around(y, o)], y_peers[k]
            copies.append(
                copy_to(part, r_one.at[i, k], sone_ss.at[i, k], sone_rs.at[i, k], target)
            )
        return copies

    def second_copies(i):
        copies = []
        for k, o in enumerate((1, 2, 3)):
            if i % 2 == 0:
                part, target = mid.at[i, around(y, o)], y_peers[k]
            else:
                part, target = mid.at[i, around(x, o)], x_peers[k]
            copies.append(
                copy_to(part, r_two.at[i, k], stwo_ss.at[i, k], stwo_rs.at[i, k], target)
            )
        return copies

    def pair_copy(i):
        return copy_to(z_send.at[i], z_recv.at[i], z_ss.at[i], z_rs.at[i], z_pair)

    def share_copies(number):
        part = owned.at[me, pl.ds(0, 4)] if number == 0 else owned.at[me, pl.ds(4, 2)]
        return [
            copy_to(part, part, share_ss.at[number, k], share_rs.at[number, k], group[k])
            for k in range(3)
        ]

    def share_arrived(number):
        for k in range(3):
            at = group_ids[k]
            part = owned.at[at, pl.ds(0, 4)] if number == 0 else owned.at[at, pl.ds(4, 2)]
            copy_to(
                part, part, share_ss.at[number, k], share_rs.at[number, k], group[k]
            ).wait_recv()

    def first_sum(i):
        for item in first_copies(i):
            item.wait_recv()

        @pl.loop(0, 4)
        def _(j):
            own = grads[i, x, j] if i % 2 == 0 else grads[i, j, y]
            total = own.astype(F32)
            for k in range(3):
                total = total + r_one[i, k, j].astype(F32)
            mid[i, j] = total.astype(BF)

        start(second_copies(i))

    def second_sum(i):
        for item in second_copies(i):
            item.wait_recv()
        total = mid[i, y if i % 2 == 0 else x].astype(F32)
        for k in range(3):
            total = total + r_two[i, k].astype(F32)
        first = z_lo == 0
        kept[i] = jnp.where(first, total[:24], total[24:])
        z_send[i] = jnp.where(first, total[24:], total[:24]).astype(BF)
        pair_copy(i).start()

    def third_sum(i):
        pair_copy(i).wait_recv()
        owned[me, i] = (kept[i] + z_recv[i].astype(F32)).astype(BF)

    def p_copies(sent, received, number):
        return [
            copy_to(
                sent.at[group_ids[k]],
                received.at[me],
                p_ss.at[number, k],
                p_rs.at[number, k],
                group[k],
            )
            for k in range(3)
        ]

    def p_arrived(sent, received, number):
        for k in range(3):
            copy_to(
                sent.at[0],
                received.at[group_ids[k]],
                p_ss.at[number, k],
                p_rs.at[number, k],
                group[k],
            ).wait_recv()

    for b in range(2):
        weight_up = weight_rows(weights.at[b])
        down = [
            weights[2 + half, 2 * b : 2 * b + 2].reshape(384, 384) for half in range(2)
        ]

        @pl.loop(0, 4)
        def _(step):
            rows = token_rows(step)
            up_pre = dot(in_mlp[rows, :], weight_up) + vec[7:8, b * 384 : b * 384 + 384]
            cdf = 0.5 * (1.0 + lax.erf(up_pre * (1.0 / math.sqrt(2.0))))
            act = (up_pre * cdf).astype(BF)
            density = jnp.exp(-0.5 * up_pre * up_pre) * (1.0 / math.sqrt(2.0 * math.pi))
            slope = cdf + up_pre * density
            grad_activ = dot_t(gg[rows, :384], down[0]) + dot_t(gg[rows, 384:], down[1])
            grad_up = (grad_activ * slope).astype(BF)
            activ[rows, :] = act
            low_grad[rows, :] = grad_up
            for half in range(2):
                cols = slice(half * 384, half * 384 + 384)
                out = dot(act, down[half])
                if b:
                    out = out + ob_part[rows, cols]
                ob_part[rows, cols] = out
            back = dot_t(grad_up, weight_up)
            if b:
                back = back + gim_part[rows, :]
            gim_part[rows, :] = back

        grads[b] = dot(in_mlp_t[...], low_grad[...]).astype(BF).reshape(4, 4, 48, 384)
        start(first_copies(b))
        small_b[6:7, b * 384 : b * 384 + 384] = jnp.sum(
            low_grad[...].astype(F32), axis=0, keepdims=True
        )
        activ_t = activ[...].T
        for half in range(2):
            grad_down = dot(activ_t, gg[:, half * 384 : half * 384 + 384]).astype(BF)
            grads[2 + half, 2 * b : 2 * b + 2] = grad_down.reshape(2, 4, 48, 384)
        if b == 0:
            arrived(VP, 2)
            for k in range(4):
                p_send[k] = weights[VP, k].reshape(192, 384)[:, 192:]
            start(p_copies(p_send, p_recv, 0))
            p_recv[me] = p_send[me]
    start(first_copies(2) + first_copies(3))

    grad_in = gim_part[...]
    small_b[2:3, :] = jnp.sum(grad_in * normed[...], axis=0, keepdims=True)
    small_b[3:4, :] = jnp.sum(grad_in, axis=0, keepdims=True)
    small_b[4:5, :] = jnp.sum(g_in[...].astype(F32), axis=0, keepdims=True)
    small_b[7:8, :] = jnp.zeros((1, WIDTH), F32)

    p_arrived(p_send, p_recv, 0)
    for k in range(4):
        p_rows[:, k * 192 : k * 192 + 192] = p_recv[k]
    arrived(QK, 2)

    @pl.loop(0, 4)
    def _(step):
        rows = token_rows(step)
        activations = in_attn[rows, :]
        pre = dot(activations, weight_rows(weights.at[QK])) + vec[6:7, :384]
        value_pre = dot(activations, weight_rows(weights.at[VP])[:, :192]) + vec[6:7, 384:576]
        value_pre = value_pre.astype(BF)
        grad_att = dot_t(gg[rows, :], p_rows[...]).astype(BF)
        for head in range(3):
            part = pre[:, head * 128 : head * 128 + 128]
            qk_rows[head, rows, :] = (
                part * tab[0, rows, :]
                + pltpu.roll(part, 120, 1) * tab[1, rows, :]
                + pltpu.roll(part, 8, 1) * tab[2, rows, :]
            ).astype(BF)
            at = slice(head * 64, head * 64 + 64)
            vd_rows[head, rows, :] = jnp.concatenate([value_pre[:, at], grad_att[:, at]], axis=1)

    scale = 1.0 / math.sqrt(HEAD_DIM)

    def attend(head):
        queries = qk_rows[head, :, 0:64]
        key_rows = qk_rows[head, :, 64:128]
        value_rows = vd_rows[head, :, 0:64]
        grad_rows = vd_rows[head, :, 64:128]
        dk_acc[...] = jnp.zeros((1024, HEAD_DIM), F32)
        dv_acc[...] = jnp.zeros((1024, HEAD_DIM), F32)
        dq_parts = []
        for blk in range(4):
            lo, hi = blk * 256, blk * 256 + 256
            q = queries[lo:hi]
            do = grad_rows[lo:hi]
            scores = dot_t(q, key_rows[:hi]) * scale
            row_place = lax.broadcasted_iota(jnp.int32, (256, hi), 0) + lo
            col_place = lax.broadcasted_iota(jnp.int32, (256, hi), 1)
            scores = jnp.where(row_place >= col_place, scores, MASKED)
            peak = jnp.max(scores, axis=-1, keepdims=True)
            expo = jnp.exp(scores - peak)
            probs = expo * (1.0 / jnp.sum(expo, axis=-1, keepdims=True))
            low_probs = probs.astype(BF)
            att[lo:hi, head * 64 : head * 64 + 64] = dot(low_probs, value_rows[:hi]).astype(BF)
            grad_probs = dot_t(do, value_rows[:hi])
            inner = jnp.sum(probs * grad_probs, axis=-1, keepdims=True)
            grad_scores = (probs * (grad_probs - inner)).astype(BF)
            dq_parts.append((dot(grad_scores, key_rows[:hi]) * scale).astype(BF))
            dk_acc[:hi, :] += dot_a(grad_scores, q)
            dv_acc[:hi, :] += dot_a(low_probs, do)
        dk = (dk_acc[...] * scale).astype(BF)
        dq = jnp.concatenate(dq_parts, axis=0)
        grad_v[:, head * 64 : head * 64 + 64] = dv_acc[...].astype(BF)
        part = jnp.concatenate([dq, dk], axis=1).astype(F32)
        grad_qk[:, head * 128 : head * 128 + 128] = (
            part * tab[0]
            - pltpu.roll(part, 120, 1) * tab[1]
            - pltpu.roll(part, 8, 1) * tab[2]
        ).astype(BF)

    attend(0)
    first_sum(0)
    first_sum(1)
    attend(1)
    first_sum(2)
    first_sum(3)
    second_sum(0)
    second_sum(1)
    attend(2)
    second_sum(2)
    second_sum(3)

    def grad_chunk(index, number):
        rows = token_rows(index)
        grad_in = dot_t(grad_qk[rows, :], weight_rows(weights.at[QK])) + dot_t(
            grad_v[rows, :], weight_rows(weights.at[VP])[:, :192]
        )
        bias = jnp.sum(grad_in, axis=0, keepdims=True)
        gain = jnp.sum(grad_in * normed[rows, :], axis=0, keepdims=True)
        if number:
            bias = bias + small_b[1:2, :]
            gain = gain + small_b[0:1, :]
        small_b[1:2, :] = bias
        small_b[0:1, :] = gain
        return grad_in * vec[0:1, :] + gim_part[rows, :] * vec[2:3, :]

    def out_chunk(index):
        rows = token_rows(index)
        return ob_part[rows, :] + dot(att[rows, :], p_rows[...])

    def swap(k):
        return copy_to(swap_f.at[k], swap_r.at[k], swap_ss.at[k], swap_rs.at[k], sibling)

    def far_swap(k):
        return copy_to(far_b.at[k], far_r.at[k], swap_ss.at[4 + k], swap_rs.at[4 + k], far)

    swap_f[0] = grad_chunk(group_ids[2], 0)
    swap(0).start()
    grads[QK] = dot(in_attn_t[...], grad_qk[...]).astype(BF).reshape(4, 4, 48, 384)
    start(first_copies(QK))
    grad_p = dot_a(att[...], gg[...]).astype(BF)
    for k in range(4):
        pg_send[k] = grad_p[:, k * 192 : k * 192 + 192]
    start(p_copies(pg_send, pg_recv, 1))
    pg_recv[me] = pg_send[me]
    near_sum = grad_chunk(group_ids[1], 1)
    swap(0).wait_recv()
    far_b[0] = (near_sum + swap_r[0]).astype(BF)
    far_swap(0).start()
    swap_f[1] = out_chunk(group_ids[2])
    swap(1).start()
    for i in range(4):
        third_sum(i)
    start(share_copies(0))
    grad_value_w = dot(in_attn_t[...], grad_v[...]).astype(BF)
    p_arrived(pg_send, pg_recv, 1)
    for k in range(4):
        grads[VP, k] = jnp.concatenate(
            [grad_value_w[k * 192 : k * 192 + 192], pg_recv[k]], axis=1
        ).reshape(4, 48, 384)
    start(first_copies(VP))
    out_sum = out_chunk(group_ids[1])
    swap(1).wait_recv()
    far_b[1] = (out_sum + swap_r[1]).astype(BF)
    far_swap(1).start()
    swap_f[2] = grad_chunk(group_ids[0], 2)
    swap(2).start()
    swap_f[3] = out_chunk(group_ids[0])
    swap(3).start()
    sums[0] = grad_chunk(me, 3)
    sums[1] = out_chunk(me)
    small_b[5:6, 0:384] = jnp.sum(grad_qk[...].astype(F32), axis=0, keepdims=True)
    small_b[5:6, 384:576] = jnp.sum(grad_v[...].astype(F32), axis=0, keepdims=True)
    small_b[5:6, 576:768] = jnp.zeros((1, 192), F32)

    def small_copies(number):
        peers = (x_peers, y_peers, [z_pair])[number]
        return [
            copy_to(
                small_r.at[7 + number],
                small_r.at[number * 3 + k],
                small_ss.at[number, k],
                small_rs.at[number, k],
                peers[k],
            )
            for k in range(len(peers))
        ]

    def small_sum(number):
        total = small_r[7 + number]
        for k, item in enumerate(small_copies(number)):
            item.wait_recv()
            total = total + small_r[number * 3 + k]
        return total

    def small_share(k):
        return copy_to(
            small.at[me], small.at[me], small_ss.at[3, k], small_rs.at[3, k], group[k]
        )

    small_r[7] = small_b[...]
    start(small_copies(0))
    first_sum(QK)
    small_r[8] = small_sum(0)
    start(small_copies(1))
    first_sum(VP)
    second_sum(QK)
    small_r[9] = small_sum(1)
    start(small_copies(2))
    second_sum(VP)
    small[me] = small_sum(2)
    for k in range(3):
        small_share(k).start()
    third_sum(QK)
    third_sum(VP)
    start(share_copies(1))

    swap(2).wait_recv()
    far_swap(0).wait_recv()
    values = x_in[...].astype(F32)
    center = values - jnp.mean(values, axis=-1, keepdims=True)
    inv_std = lax.rsqrt(jnp.mean(center * center, axis=-1, keepdims=True) + EPSILON)
    norm_rows = center * inv_std
    grad_norm = sums[0] + swap_r[2] + far_r[0].astype(F32)
    input_grad[...] = (
        g_in[...].astype(F32)
        + inv_std
        * (
            grad_norm
            - jnp.mean(grad_norm, axis=-1, keepdims=True)
            - norm_rows * jnp.mean(grad_norm * norm_rows, axis=-1, keepdims=True)
        )
    ).astype(BF)
    swap(3).wait_recv()
    far_swap(1).wait_recv()
    block_out[...] = (
        values + sums[1] + swap_r[3] + far_r[1].astype(F32) + (vec[4:5, :] + vec[5:6, :])
    ).astype(BF)

    share_arrived(0)
    share_arrived(1)
    for k in range(3):
        copy_to(
            small.at[group_ids[k]],
            small.at[group_ids[k]],
            small_ss.at[3, k],
            small_rs.at[3, k],
            group[k],
        ).wait_recv()
    sent = pair + [item for three in tokens for item in three]
    for i in range(N_BLOCK + 1):
        sent += gather(i, 1) + gather(i, 2)
    for i in range(N_BLOCK):
        sent += first_copies(i) + second_copies(i) + [pair_copy(i)]
    sent += p_copies(p_send, p_recv, 0) + p_copies(pg_send, pg_recv, 1)
    sent += share_copies(0) + share_copies(1) + [small_share(k) for k in range(3)]
    sent += [swap(k) for k in range(4)] + [far_swap(k) for k in range(2)]
    for number in range(3):
        sent += small_copies(number)
    for item in sent:
        item.wait_send()


def whole(x_in, g_in, w_a, vec_in, tab):
    shape = jax.ShapeDtypeStruct
    outs = (
        shape((256, WIDTH), BF),
        shape((256, WIDTH), BF),
        shape((4, N_BLOCK, 24, 384), BF),
        shape((4, 8, WIDTH), F32),
    )
    dma = pltpu.SemaphoreType.DMA
    vmem = pl.BlockSpec(memory_space=pltpu.VMEM)
    rows = 1024
    buffers = [
        ((N_BLOCK, 4, 4, 48, 384), BF),
        ((4, 4, 16, WIDTH), BF),
        ((N_BLOCK, 24, 384), BF),
        ((16, WIDTH), BF),
        ((16, WIDTH), F32),
        ((rows, WIDTH), BF),
        ((rows, WIDTH), BF),
        ((rows, WIDTH), F32),
        ((rows, WIDTH), BF),
        ((WIDTH, rows), BF),
        ((rows, WIDTH), BF),
        ((WIDTH, rows), BF),
        ((rows, 384), BF),
        ((rows, 384), BF),
        ((rows, WIDTH), F32),
        ((rows, WIDTH), F32),
        ((N_BLOCK, 4, 4, 48, 384), BF),
        ((4, 192, 192), BF),
        ((4, 192, 192), BF),
        ((192, WIDTH), BF),
        ((3, rows, 128), BF),
        ((3, rows, 128), BF),
        ((rows, HEAD_DIM), F32),
        ((rows, HEAD_DIM), F32),
        ((rows, 192), BF),
        ((rows, 384), BF),
        ((rows, 192), BF),
        ((4, 192, 192), BF),
        ((4, 192, 192), BF),
        ((N_BLOCK, 3, 4, 48, 384), BF),
        ((N_BLOCK, 4, 48, 384), BF),
        ((N_BLOCK, 3, 48, 384), BF),
        ((N_BLOCK, 24, 384), F32),
        ((N_BLOCK, 24, 384), BF),
        ((N_BLOCK, 24, 384), BF),
        ((2, 256, WIDTH), F32),
        ((4, 256, WIDTH), F32),
        ((4, 256, WIDTH), F32),
        ((2, 256, WIDTH), BF),
        ((2, 256, WIDTH), BF),
        ((8, WIDTH), F32),
        ((10, 8, WIDTH), F32),
    ]
    sems = [
        (4,),
        (2, 3),
        (N_BLOCK + 1, 3),
        (N_BLOCK + 1, 3),
        (2, 3),
        (N_BLOCK, 3),
        (N_BLOCK, 3),
        (N_BLOCK,),
        (2, 3),
        (6,),
        (4, 3),
    ]
    scratch = [pltpu.VMEM(*item) for item in buffers]
    for item in sems:
        scratch += [dma(item), dma(item)]
    return pl.pallas_call(
        whole_kernel,
        name="whole",
        out_shape=outs,
        in_specs=[vmem] * 5,
        out_specs=(vmem,) * len(outs),
        scratch_shapes=scratch,
        compiler_params=pltpu.CompilerParams(
            collective_id=0, has_side_effects=True, vmem_limit_bytes=60 * MIB
        ),
    )(x_in, g_in, w_a, vec_in, tab)


def finish_kernel(
    out_in,
    grad_in,
    owned,
    small,
    block_out,
    input_grad,
    attn_gain_g,
    attn_bias_g,
    mlp_gain_g,
    mlp_bias_g,
    qkv_g,
    qkv_bias_g,
    proj_g,
    proj_bias_g,
    up_g,
    up_bias_g,
    down_g,
    down_bias_g,
):
    block_out[...] = out_in[...]
    input_grad[...] = grad_in[...]
    up_parts = []
    for g in range(4):
        qk = owned[g, QK].astype(F32)
        vp = owned[g, VP].astype(F32)
        for head in range(3):
            at = 576 * g + 192 * head
            qkv_g[:, at : at + 128] = qk[:, head * 128 : head * 128 + 128]
            qkv_g[:, at + 128 : at + 192] = vp[:, head * 64 : head * 64 + 64]
        proj_g[:, 192 * g : 192 * g + 192] = vp[:, 192:]
        for half in range(2):
            down_g[24 * g : 24 * g + 24, half * 384 : half * 384 + 384] = owned[
                g, 2 + half
            ].astype(F32)
        up_parts.append([owned[g, 0].astype(F32), owned[g, 1].astype(F32)])
    for d in range(32):
        at = (d % 16) * 24
        up_g[:, 96 * d : 96 * d + 96] = jnp.concatenate(
            [up_parts[g][d // 16][:, at : at + 24] for g in range(4)], axis=1
        )

    dp = lax.axis_index("dp")
    totals = small[0] + small[1] + small[2] + small[3]
    rows = jnp.concatenate(
        [totals] + [small[g, 6:7, :] for g in range(4)] + [jnp.zeros((4, WIDTH), F32)], axis=0
    )

    def pick(values, each):
        size = values.shape[1]
        row = lax.broadcasted_iota(jnp.int32, (size, each), 0)
        col = lax.broadcasted_iota(jnp.int32, (size, each), 1)
        chosen = (row == col + dp * each).astype(F32)
        return jnp.dot(
            values, chosen, precision=lax.Precision.HIGHEST, preferred_element_type=F32
        )

    picked = pick(rows, 24)
    attn_gain_g[...] = picked[0:1]
    attn_bias_g[...] = picked[1:2]
    mlp_gain_g[...] = picked[2:3]
    mlp_bias_g[...] = picked[3:4]
    proj_bias_g[...] = picked[4:5]
    down_bias_g[...] = picked[4:5]
    up_bias_g[...] = jnp.concatenate([picked[8 + g : 9 + g] for g in range(4)], axis=1)
    pieces = []
    for g in range(4):
        for head in range(3):
            pieces.append(small[g, 5:6, head * 128 : head * 128 + 128])
            pieces.append(small[g, 5:6, 384 + head * 64 : 384 + head * 64 + 64])
    bias = jnp.concatenate(pieces, axis=1)
    qkv_bias_g[...] = pick(jnp.broadcast_to(bias, (8, 2304)), 72)[0:1]


def finish(out_in, grad_in, owned, small):
    shape = jax.ShapeDtypeStruct
    outs = (
        shape((256, WIDTH), BF),
        shape((256, WIDTH), BF),
        shape((1, 24), F32),
        shape((1, 24), F32),
        shape((1, 24), F32),
        shape((1, 24), F32),
        shape((24, 2304), F32),
        shape((1, 72), F32),
        shape((24, 768), F32),
        shape((1, 24), F32),
        shape((24, 3072), F32),
        shape((1, 96), F32),
        shape((96, 768), F32),
        shape((1, 24), F32),
    )
    vmem = pl.BlockSpec(memory_space=pltpu.VMEM)
    return pl.pallas_call(
        finish_kernel,
        name="finish",
        out_shape=outs,
        in_specs=[vmem] * 4,
        out_specs=(vmem,) * len(outs),
        compiler_params=pltpu.CompilerParams(vmem_limit_bytes=32 * MIB),
    )(out_in, grad_in, owned, small)


def rotary_tables():
    half = ROT_DIM // 2
    freqs = np.power(np.float32(10000.0), np.float32(-2.0) * np.arange(half, dtype=np.float32) / np.float32(ROT_DIM))
    angles = np.arange(1024, dtype=np.float32)[:, None] * freqs.astype(np.float32)[None, :]
    cosine, sine = np.cos(angles), np.sin(angles)
    ones = np.ones((1024, HEAD_DIM - ROT_DIM), np.float32)
    zero = np.zeros((1024, half), np.float32)
    cos_row = np.concatenate([cosine, cosine, ones], axis=1)
    left = np.concatenate([-sine, zero, ones * 0.0], axis=1)
    right = np.concatenate([zero, sine, ones * 0.0], axis=1)
    return np.stack([np.tile(t, (1, 2)) for t in (cos_row, left, right)]).astype(np.float32)


def place(values, owner, count):
    each = values.shape[0]
    spots = jnp.arange(count) // each
    return jnp.where(spots == owner, jnp.tile(values, count // each), jnp.zeros((), values.dtype))


def local(
    block_in,
    cotangent,
    attn_gain,
    attn_bias,
    mlp_gain,
    mlp_bias,
    qkv_weight,
    qkv_bias,
    proj_weight,
    proj_bias,
    up_weight,
    up_bias,
    down_weight,
    down_bias,
):
    dp = lax.axis_index("dp")
    me = lax.axis_index("seq")

    def quarter(array, axis):
        return lax.dynamic_index_in_dim(array, me, axis, keepdims=False)

    qkv = quarter(qkv_weight.reshape(24, 4, 3, 3, HEAD_DIM), 1)
    w_qk = qkv[:, :, :2, :].reshape(24, 384)
    w_v = qkv[:, :, 2, :].reshape(24, 192)
    w_p = quarter(proj_weight.reshape(24, 4, 192), 1)
    w_u = quarter(up_weight.reshape(24, 32, 4, 24), 2).reshape(24, 2, 384).transpose(1, 0, 2)
    w_d = quarter(down_weight.reshape(4, 24, 2, 384), 0).transpose(1, 0, 2)
    w_a = jnp.concatenate(
        [w_u, w_d, w_qk[None], jnp.concatenate([w_v, w_p], axis=1)[None]], axis=0
    )
    b_qkv = quarter(place(qkv_bias, dp, 2304).reshape(4, 3, 3, HEAD_DIM), 0)
    b_qkv = jnp.concatenate(
        [b_qkv[:, :2].reshape(384), b_qkv[:, 2].reshape(192), jnp.zeros((192,), BF)]
    )
    b_u = quarter(place(up_bias, dp, 3072).reshape(32, 4, 24), 1).reshape(768)
    rows = [
        place(v, dp, 768)
        for v in (attn_gain, attn_bias, mlp_gain, mlp_bias, proj_bias, down_bias)
    ]
    vec_in = jnp.concatenate([jnp.stack(rows + [b_qkv, b_u]), jnp.zeros((8, 768), BF)])
    out, grad, owned, small = whole(
        block_in.reshape(256, WIDTH),
        cotangent.reshape(256, WIDTH),
        w_a,
        vec_in,
        jnp.asarray(rotary_tables()),
    )
    results = finish(out, grad, owned, small)
    shapes = [(1, 256, WIDTH)] * 2 + [(24,)] * 4
    shapes += [(24, 2304), (72,), (24, 768), (24,), (24, 3072), (96,), (96, 768), (24,)]
    return tuple(value.reshape(size) for value, size in zip(results, shapes))


def solution(mesh):
    tokens = P("dp", "seq", None)
    in_specs = (tokens, tokens) + (P("dp"),) * 4 + (P("dp", None), P("dp")) * 4
    return jax.shard_map(
        local, mesh=mesh, in_specs=in_specs, out_specs=in_specs, check_vma=False
    )
```

```python
import math

import jax
import jax.numpy as jnp
import numpy as np
from jax import lax
from jax.experimental import pallas as pl
from jax.experimental.pallas import tpu as pltpu
from jax.sharding import PartitionSpec as P

HEADS = 12
HEAD_DIM = 64
ROT_DIM = 16
WIDTH = 768
EPSILON = 1e-05
MASKED = -1e30
MESH = pl.DeviceIdType.MESH
BF = jnp.bfloat16
F32 = jnp.float32
MIB = 1 << 20


def coords():
    dp = lax.axis_index("dp")
    seq = lax.axis_index("seq")
    x = lax.div(dp, 8)
    y = lax.rem(lax.div(dp, 2), 4)
    z_lo = lax.rem(dp, 2)
    z_hi = lax.div(seq, 2)
    core = lax.rem(seq, 2)
    return x, y, z_hi * 2 + z_lo, core


def device(x, y, z, core):
    return (x * 8 + y * 2 + lax.rem(z, 2), lax.div(z, 2) * 2 + core)


def around(at, offset):
    return lax.rem(at + offset, 4)


def copy_to(src, dst, send_sem, recv_sem, target):
    return pltpu.make_async_remote_copy(
        src_ref=src,
        dst_ref=dst,
        send_sem=send_sem,
        recv_sem=recv_sem,
        device_id=target,
        device_id_type=MESH,
    )


def dot(left, right):
    return jnp.dot(left, right, preferred_element_type=F32)


def dot_t(left, right):
    return lax.dot_general(left, right, (((1,), (1,)), ((), ())), preferred_element_type=F32)


def dot_a(left, right):
    return lax.dot_general(left, right, (((0,), (0,)), ((), ())), preferred_element_type=F32)


def one_hot(rows, cols, chosen):
    row = lax.broadcasted_iota(jnp.int32, (rows, cols), 0)
    col = lax.broadcasted_iota(jnp.int32, (rows, cols), 1)
    return chosen(row, col).astype(F32).astype(BF)


def weight_rows(ref):
    value = ref[...]
    return value.reshape(value.shape[0] * value.shape[1] * value.shape[2], value.shape[3])


def slab_rows(value):
    return value.reshape(value.shape[0] * value.shape[1], value.shape[2])


N_BLOCK = 6
QK, VP = 4, 5


def whole_kernel(
    x_in,
    g_in,
    qkv_weight,
    proj_weight,
    up_weight,
    down_weight,
    vec_raw,
    tab_in,
    block_out,
    input_grad,
    owned,
    small,
    qkv_own,
    proj_own,
    up_own,
    down_own,
    vec_own,
    tab,
    w_a,
    vec_in,
    weights,
    vecs,
    z_a,
    z_v,
    vec,
    xx,
    gg,
    normed,
    in_attn,
    in_attn_t,
    in_mlp,
    in_mlp_t,
    activ,
    activ_t,
    ob_part,
    gim_part,
    grads,
    p_send,
    p_recv,
    p_rows,
    p_far,
    p_far_rows,
    att_send,
    att_recv,
    qk_rows,
    vd_rows,
    dk_acc,
    dv_acc,
    att,
    grad_qk,
    grad_v,
    pg_send,
    pg_recv,
    r_one,
    mid,
    r_two,
    kept,
    z_send,
    z_recv,
    swap_f,
    swap_r,
    far_b,
    far_r,
    small_b,
    small_r,
    load_sem,
    pair_ss,
    pair_rs,
    tok_ss,
    tok_rs,
    one_ss,
    one_rs,
    two_ss,
    two_rs,
    p_ss,
    p_rs,
    sone_ss,
    sone_rs,
    stwo_ss,
    stwo_rs,
    z_ss,
    z_rs,
    share_ss,
    share_rs,
    swap_ss,
    swap_rs,
    small_ss,
    small_rs,
):
    x, y, z, core = coords()
    z_lo = lax.rem(z, 2)
    z_hi = lax.div(z, 2)
    me = z_hi * 2 + core
    x_peers = [device(around(x, o), y, z, core) for o in (1, 2, 3)]
    y_peers = [device(x, around(y, o), z, core) for o in (1, 2, 3)]
    z_far = around(z, 2)
    sibling = device(x, y, z, 1 - core)
    far = device(x, y, z_far, core)
    cross = device(x, y, z_far, 1 - core)
    z_pair = device(x, y, z_hi * 2 + 1 - z_lo, core)
    group = [sibling, far, cross]
    group_ids = [z_hi * 2 + 1 - core, (1 - z_hi) * 2 + core, (1 - z_hi) * 2 + 1 - core]
    barrier = pltpu.get_barrier_semaphore()
    everyone = x_peers + y_peers + group + [z_pair]
    for target in everyone:
        pl.semaphore_signal(barrier, inc=1, device_id=target, device_id_type=MESH)

    def token_rows(index):
        return pl.ds(pl.multiple_of(index * 256, 256), 256)

    def start(copies):
        for item in copies:
            item.start()

    mine = token_rows(me)
    theirs = token_rows(group_ids[1])
    loads = [
        pltpu.make_async_copy(source, held, load_sem.at[k])
        for k, (source, held) in enumerate(
            (
                (up_weight, up_own),
                (down_weight, down_own),
                (vec_raw, vec_own),
                (qkv_weight, qkv_own),
                (proj_weight, proj_own),
                (x_in, xx.at[mine]),
                (g_in, gg.at[mine]),
                (tab_in, tab),
            )
        )
    ]
    for item in loads:
        item.start()

    def of_quarter(parts):
        value = parts[3]
        for k in (2, 1, 0):
            value = jnp.where(me == k, parts[k], value)
        return value

    loads[0].wait()
    chosen = one_hot(
        384,
        96,
        lambda row, col: row
        == col
        + 24 * me
        + 72 * ((col >= 24).astype(jnp.int32) + (col >= 48).astype(jnp.int32) + (col >= 72).astype(jnp.int32)),
    )
    for b in range(2):
        w_a[b] = jnp.concatenate(
            [dot(up_own[:, k * 384 : k * 384 + 384], chosen) for k in range(4 * b, 4 * b + 4)],
            axis=1,
        ).astype(BF)
    loads[1].wait()
    picked = dot(one_hot(24, 96, lambda row, col: col == row + 24 * me), down_own[...])
    w_a[2] = picked[:, :384].astype(BF)
    w_a[3] = picked[:, 384:].astype(BF)
    loads[2].wait()
    owner = lax.axis_index("dp")
    raw = vec_own[...].astype(F32)
    up_bias = of_quarter([raw[7:8, 24 * k : 24 * k + 24] for k in range(4)])
    eight = jnp.concatenate([raw[:7, :24], up_bias], axis=0).astype(BF)
    placed = dot(eight, one_hot(24, WIDTH, lambda row, col: col == row + 24 * owner))
    start_at = jnp.where(x == me, 72 * lax.rem(owner, 8), 2 * WIDTH)
    placed_qkv = dot(
        jnp.broadcast_to(raw[6:7, :72], (8, 72)).astype(BF),
        one_hot(72, WIDTH, lambda row, col: col == row + start_at),
    )
    vec_in[...] = jnp.concatenate(
        [placed[:6], placed_qkv[:1], placed[7:], jnp.zeros((8, WIDTH), F32)], axis=0
    ).astype(BF)
    loads[3].wait()
    loads[4].wait()
    qkv_f = qkv_own[...].astype(F32)
    proj_f = proj_own[...].astype(F32)
    w_a[QK] = jnp.concatenate(
        [
            of_quarter([qkv_f[:, 576 * k + 192 * h : 576 * k + 192 * h + 128] for k in range(4)])
            for h in range(3)
        ],
        axis=1,
    ).astype(BF)
    w_a[VP] = jnp.concatenate(
        [
            of_quarter([qkv_f[:, 576 * k + 192 * h + 128 : 576 * k + 192 * h + 192] for k in range(4)])
            for h in range(3)
        ]
        + [of_quarter([proj_f[:, 192 * k : 192 * k + 192] for k in range(4)])],
        axis=1,
    ).astype(BF)
    pl.semaphore_wait(barrier, len(everyone))

    pair = [copy_to(vec_in, z_v, pair_ss.at[0], pair_rs.at[0], z_pair)]
    for k in range(3):
        part = pl.ds(2 * k, 2)
        pair.append(
            copy_to(w_a.at[part], z_a.at[part], pair_ss.at[1 + k], pair_rs.at[1 + k], z_pair)
        )
    start([pair[1], pair[0], pair[2], pair[3]])

    tokens = []
    for k, (source, held) in enumerate(((x_in, xx), (g_in, gg))):
        tokens.append(
            (
                copy_to(source, held.at[mine], tok_ss.at[k, 0], tok_rs.at[k, 0], sibling),
                copy_to(source, held.at[mine], tok_ss.at[k, 1], tok_rs.at[k, 1], far),
                copy_to(held.at[theirs], held.at[theirs], tok_ss.at[k, 2], tok_rs.at[k, 2], sibling),
            )
        )
    for k in range(2):
        tokens[k][1].start()
        tokens[k][0].start()

    def assemble(i):
        own = w_a[i].astype(F32)
        other = z_a[i].astype(F32)
        first = z_lo == 0
        weights[i, x, y] = jnp.concatenate(
            [jnp.where(first, own, other), jnp.where(first, other, own)], axis=0
        ).astype(BF)

    def gather_ref(i):
        return vecs if i == N_BLOCK else weights.at[i]

    def gather(i, number, arriving=False):
        ref = gather_ref(i)
        along_y = (i % 2 == 0) == (number == 1)
        ss, rs = (one_ss, one_rs) if number == 1 else (two_ss, two_rs)
        copies = []
        for k, o in enumerate((1, 2, 3)):
            target = y_peers[k] if along_y else x_peers[k]
            xs, ys = x, y
            if arriving and along_y:
                ys = around(y, 4 - o)
            elif arriving:
                xs = around(x, 4 - o)
            if number == 1:
                part = ref.at[xs, ys]
            elif along_y:
                part = ref.at[:, ys]
            else:
                part = ref.at[xs]
            copies.append(copy_to(part, part, ss.at[i, k], rs.at[i, k], target))
        return copies

    def arrived(i, number):
        for item in gather(i, number, True):
            item.wait_recv()

    def layer_norm(index):
        for step in range(2):
            rows = pl.ds(pl.multiple_of(index * 256 + step * 128, 128), 128)
            values = xx[rows, :].astype(F32)
            center = values - jnp.mean(values, axis=-1, keepdims=True)
            inv_std = lax.rsqrt(jnp.mean(center * center, axis=-1, keepdims=True) + EPSILON)
            normed[rows, :] = center * inv_std

    def norm_inputs(index):
        rows = token_rows(index)
        values = normed[rows, :]
        attn_rows = (values * vec[0:1, :] + vec[1:2, :]).astype(BF)
        mlp_rows = (values * vec[2:3, :] + vec[3:4, :]).astype(BF)
        in_attn[rows, :] = attn_rows
        in_mlp[rows, :] = mlp_rows
        in_attn_t[:, rows] = attn_rows.T
        in_mlp_t[:, rows] = mlp_rows.T

    pair[1].wait_recv()
    assemble(0)
    assemble(1)
    start(gather(0, 1) + gather(1, 1))
    pair[0].wait_recv()
    vecs[x, y] = (vec_in[...].astype(F32) + z_v[...].astype(F32)).astype(BF)
    start(gather(N_BLOCK, 1))
    pair[2].wait_recv()
    assemble(2)
    assemble(3)
    start(gather(2, 1) + gather(3, 1))
    for i in (0, 1, N_BLOCK):
        arrived(i, 1)
        start(gather(i, 2))
    pair[3].wait_recv()
    assemble(4)
    assemble(5)
    start(gather(4, 1) + gather(5, 1))
    loads[5].wait()
    layer_norm(me)
    for i in (2, 3, 4, 5):
        arrived(i, 1)
        start(gather(i, 2))
    tokens[0][0].wait_recv()
    layer_norm(group_ids[0])
    arrived(N_BLOCK, 2)
    total = jnp.zeros((16, WIDTH), F32)
    for i in range(4):
        for j in range(4):
            total = total + vecs[i, j].astype(F32)
    vec[...] = total
    norm_inputs(me)
    norm_inputs(group_ids[0])
    tokens[0][1].wait_recv()
    tokens[0][2].start()
    layer_norm(group_ids[1])
    norm_inputs(group_ids[1])
    tokens[0][2].wait_recv()
    layer_norm(group_ids[2])
    norm_inputs(group_ids[2])
    arrived(0, 2)
    arrived(1, 2)

    def first_copies(i):
        ref = grads.at[i]
        copies = []
        for k, o in enumerate((1, 2, 3)):
            if i % 2 == 0:
                part, target = ref.at[around(x, o)], x_peers[k]
            else:
                part, target = ref.at[:, around(y, o)], y_peers[k]
            copies.append(
                copy_to(part, r_one.at[i, k], sone_ss.at[i, k], sone_rs.at[i, k], target)
            )
        return copies

    def second_copies(i):
        copies = []
        for k, o in enumerate((1, 2, 3)):
            if i % 2 == 0:
                part, target = mid.at[i, around(y, o)], y_peers[k]
            else:
                part, target = mid.at[i, around(x, o)], x_peers[k]
            copies.append(
                copy_to(part, r_two.at[i, k], stwo_ss.at[i, k], stwo_rs.at[i, k], target)
            )
        return copies

    def pair_copy(i):
        return copy_to(z_send.at[i], z_recv.at[i], z_ss.at[i], z_rs.at[i], z_pair)

    def share_copies(number):
        part = owned.at[me, pl.ds(0, 4)] if number == 0 else owned.at[me, pl.ds(4, 2)]
        return [
            copy_to(part, part, share_ss.at[number, k], share_rs.at[number, k], group[k])
            for k in range(3)
        ]

    def share_arrived(number):
        for k in range(3):
            at = group_ids[k]
            part = owned.at[at, pl.ds(0, 4)] if number == 0 else owned.at[at, pl.ds(4, 2)]
            copy_to(
                part, part, share_ss.at[number, k], share_rs.at[number, k], group[k]
            ).wait_recv()

    def first_sum(i):
        for item in first_copies(i):
            item.wait_recv()

        @pl.loop(0, 4)
        def _(j):
            own = grads[i, x, j] if i % 2 == 0 else grads[i, j, y]
            total = own.astype(F32)
            for k in range(3):
                total = total + r_one[i, k, j].astype(F32)
            mid[i, j] = total.astype(BF)

        start(second_copies(i))

    def second_sum(i):
        for item in second_copies(i):
            item.wait_recv()
        total = mid[i, y if i % 2 == 0 else x].astype(F32)
        for k in range(3):
            total = total + r_two[i, k].astype(F32)
        first = z_lo == 0
        kept[i] = jnp.where(first, total[:24], total[24:])
        z_send[i] = jnp.where(first, total[24:], total[:24]).astype(BF)
        pair_copy(i).start()

    def third_sum(i):
        pair_copy(i).wait_recv()
        owned[me, i] = (kept[i] + z_recv[i].astype(F32)).astype(BF)

    def p_copies(sent, received, number, turn=0):
        return [
            copy_to(
                sent.at[around(group_ids[k], turn)],
                received.at[me],
                p_ss.at[number, k],
                p_rs.at[number, k],
                group[k],
            )
            for k in range(3)
        ]

    def p_arrived(sent, received, number):
        for k in range(3):
            copy_to(
                sent.at[0],
                received.at[group_ids[k]],
                p_ss.at[number, k],
                p_rs.at[number, k],
                group[k],
            ).wait_recv()

    def swap(k):
        return copy_to(swap_f.at[k], swap_r.at[k], swap_ss.at[k], swap_rs.at[k], sibling)

    def far_swap(k):
        return copy_to(far_b.at[k], far_r.at[k], swap_ss.at[4 + k], swap_rs.at[4 + k], far)

    def att_copy(k):
        return copy_to(
            att_send.at[k], att_recv.at[k], swap_ss.at[6 + k], swap_rs.at[6 + k], far
        )

    @pl.loop(0, 4)
    def _(step):
        rows = token_rows(step)
        for b in range(2):
            cols = slice(b * 384, b * 384 + 384)
            up_pre = dot(in_mlp[rows, :], weight_rows(weights.at[b])) + vec[7:8, cols]
            cdf = 0.5 * (1.0 + lax.erf(up_pre * (1.0 / math.sqrt(2.0))))
            act = (up_pre * cdf).astype(BF)
            density = jnp.exp(-0.5 * up_pre * up_pre) * (1.0 / math.sqrt(2.0 * math.pi))
            activ[rows, cols] = act
            activ_t[cols, rows] = act.T
            swap_f[step, :, cols] = cdf + up_pre * density

    def mlp_back(index):
        rows = token_rows(index)
        down = [weight_rows(weights.at[2 + half]) for half in range(2)]
        grad_activ = dot_t(gg[rows, :384], down[0]) + dot_t(gg[rows, 384:], down[1])
        grad_up = (grad_activ * swap_f[index]).astype(BF)
        act = activ[rows, :]
        activ[rows, :] = grad_up
        for half in range(2):
            cols = slice(half * 384, half * 384 + 384)
            ob_part[rows, cols] = dot(act, down[half])
        gim_part[rows, :] = dot_t(grad_up[:, :384], weight_rows(weights.at[0])) + dot_t(
            grad_up[:, 384:], weight_rows(weights.at[1])
        )

    loads[6].wait()
    tokens[1][0].wait_recv()
    arrived(2, 2)
    arrived(3, 2)

    @pl.loop(0, 2)
    def _(step):
        mlp_back(z_hi * 2 + step)

    tokens[1][1].wait_recv()
    tokens[1][2].start()
    arrived(VP, 2)
    for k in range(4):
        p_send[k] = weights[VP, k].reshape(192, 384)[:, 192:]
    start(p_copies(p_send, p_recv, 0) + p_copies(p_send, p_far, 2, 2))
    p_recv[me] = p_send[me]
    p_far[me] = p_send[around(me, 2)]
    tokens[1][2].wait_recv()
    for half in range(2):
        cols = slice(half * 384, half * 384 + 384)
        grads[2 + half] = dot(activ_t[...], gg[:, cols]).astype(BF).reshape(4, 4, 48, 384)
        start(first_copies(2 + half))

    @pl.loop(0, 2)
    def _(step):
        mlp_back((1 - z_hi) * 2 + step)

    for b in range(2):
        cols = slice(b * 384, b * 384 + 384)
        grads[b] = dot(in_mlp_t[...], activ[:, cols]).astype(BF).reshape(4, 4, 48, 384)
        start(first_copies(b))
    swap_f[1] = ob_part[token_rows(group_ids[2]), :]
    swap(1).start()
    small_b[6:7, :] = jnp.sum(activ[...].astype(F32), axis=0, keepdims=True)
    grad_in = gim_part[...]
    small_b[2:3, :] = jnp.sum(grad_in * normed[...], axis=0, keepdims=True)
    small_b[3:4, :] = jnp.sum(grad_in, axis=0, keepdims=True)
    small_b[4:5, :] = jnp.sum(gg[mine, :].astype(F32), axis=0, keepdims=True)
    small_b[7:8, :] = jnp.zeros((1, WIDTH), F32)

    p_arrived(p_send, p_recv, 0)
    p_arrived(p_send, p_far, 2)
    for k in range(4):
        p_rows[:, k * 192 : k * 192 + 192] = p_recv[k]
        p_far_rows[:, k * 192 : k * 192 + 192] = p_far[k]
    arrived(QK, 2)
    loads[7].wait()

    @pl.loop(0, 4)
    def _(step):
        rows = token_rows(step)
        activations = in_attn[rows, :]
        bias = vec[6:7, :576]
        pre = dot(activations, weight_rows(weights.at[QK])) + jnp.concatenate(
            [bias[:, 192 * h : 192 * h + 128] for h in range(3)], axis=1
        )
        value_pre = dot(activations, weight_rows(weights.at[VP])[:, :192]) + jnp.concatenate(
            [bias[:, 192 * h + 128 : 192 * h + 192] for h in range(3)], axis=1
        )
        value_pre = value_pre.astype(BF)
        grad_att = dot_t(gg[rows, :], p_rows[...]).astype(BF)
        for head in range(3):
            part = pre[:, head * 128 : head * 128 + 128]
            qk_rows[head, rows, :] = (
                part * tab[0, rows, :]
                + pltpu.roll(part, 120, 1) * tab[1, rows, :]
                + pltpu.roll(part, 8, 1) * tab[2, rows, :]
            ).astype(BF)
            at = slice(head * 64, head * 64 + 64)
            vd_rows[head, rows, :] = jnp.concatenate([value_pre[:, at], grad_att[:, at]], axis=1)

    scale = 1.0 / math.sqrt(HEAD_DIM)

    def attend(head):
        queries = qk_rows[head, :, 0:64]
        key_rows = qk_rows[head, :, 64:128]
        value_rows = vd_rows[head, :, 0:64]
        grad_rows = vd_rows[head, :, 64:128]
        dk_acc[...] = jnp.zeros((1024, HEAD_DIM), F32)
        dv_acc[...] = jnp.zeros((1024, HEAD_DIM), F32)
        dq_parts = []
        for blk in range(4):
            lo, hi = blk * 256, blk * 256 + 256
            q = queries[lo:hi]
            do = grad_rows[lo:hi]
            scores = dot_t(q, key_rows[:hi]) * scale
            row_place = lax.broadcasted_iota(jnp.int32, (256, hi), 0) + lo
            col_place = lax.broadcasted_iota(jnp.int32, (256, hi), 1)
            scores = jnp.where(row_place >= col_place, scores, MASKED)
            peak = jnp.max(scores, axis=-1, keepdims=True)
            expo = jnp.exp(scores - peak)
            probs = expo * (1.0 / jnp.sum(expo, axis=-1, keepdims=True))
            low_probs = probs.astype(BF)
            att[lo:hi, head * 64 : head * 64 + 64] = dot(low_probs, value_rows[:hi]).astype(BF)
            grad_probs = dot_t(do, value_rows[:hi])
            inner = jnp.sum(probs * grad_probs, axis=-1, keepdims=True)
            grad_scores = (probs * (grad_probs - inner)).astype(BF)
            dq_parts.append((dot(grad_scores, key_rows[:hi]) * scale).astype(BF))
            dk_acc[:hi, :] += dot_a(grad_scores, q)
            dv_acc[:hi, :] += dot_a(low_probs, do)
        dk = (dk_acc[...] * scale).astype(BF)
        dq = jnp.concatenate(dq_parts, axis=0)
        grad_v[:, head * 64 : head * 64 + 64] = dv_acc[...].astype(BF)
        part = jnp.concatenate([dq, dk], axis=1).astype(F32)
        grad_qk[:, head * 128 : head * 128 + 128] = (
            part * tab[0]
            - pltpu.roll(part, 120, 1) * tab[1]
            - pltpu.roll(part, 8, 1) * tab[2]
        ).astype(BF)

    swap(1).wait_recv()
    far_b[1] = (ob_part[token_rows(group_ids[1]), :] + swap_r[1]).astype(BF)
    far_swap(1).start()
    far_rows = pl.ds(pl.multiple_of((1 - z_hi) * 512, 512), 512)
    attend(0)
    first_sum(2)
    first_sum(3)
    attend(1)
    att_send[0] = att[far_rows, 0:128]
    att_copy(0).start()
    first_sum(0)
    first_sum(1)
    second_sum(2)
    second_sum(3)
    attend(2)
    att_send[1] = jnp.concatenate([att[far_rows, 128:192], jnp.zeros((512, 64), BF)], axis=1)
    att_copy(1).start()
    second_sum(0)
    second_sum(1)

    def grad_chunk(index, number):
        rows = token_rows(index)
        grad_in = dot_t(grad_qk[rows, :], weight_rows(weights.at[QK])) + dot_t(
            grad_v[rows, :], weight_rows(weights.at[VP])[:, :192]
        )
        bias = jnp.sum(grad_in, axis=0, keepdims=True)
        gain = jnp.sum(grad_in * normed[rows, :], axis=0, keepdims=True)
        if number:
            bias = bias + small_b[1:2, :]
            gain = gain + small_b[0:1, :]
        small_b[1:2, :] = bias
        small_b[0:1, :] = gain
        return grad_in * vec[0:1, :] + gim_part[rows, :] * vec[2:3, :]

    def out_chunk(index):
        rows = token_rows(index)
        near = pl.ds(pl.multiple_of((index - 2 * z_hi) * 256, 256), 256)
        far_heads = jnp.concatenate([att_recv[0, near, :], att_recv[1, near, 0:64]], axis=1)
        return (
            ob_part[rows, :] + dot(att[rows, :], p_rows[...]) + dot(far_heads, p_far_rows[...])
        )

    grads[QK] = dot(in_attn_t[...], grad_qk[...]).astype(BF).reshape(4, 4, 48, 384)
    start(first_copies(QK))
    swap_f[0] = grad_chunk(group_ids[2], 0)
    swap(0).start()
    grad_p = dot_a(att[...], gg[...]).astype(BF)
    for k in range(4):
        pg_send[k] = grad_p[:, k * 192 : k * 192 + 192]
    start(p_copies(pg_send, pg_recv, 1))
    pg_recv[me] = pg_send[me]
    near_sum = grad_chunk(group_ids[1], 1)
    swap(0).wait_recv()
    far_b[0] = (near_sum + swap_r[0]).astype(BF)
    far_swap(0).start()
    for i in range(4):
        third_sum(i)
    start(share_copies(0))
    grad_value_w = dot(in_attn_t[...], grad_v[...]).astype(BF)
    p_arrived(pg_send, pg_recv, 1)
    for k in range(4):
        grads[VP, k] = jnp.concatenate(
            [grad_value_w[k * 192 : k * 192 + 192], pg_recv[k]], axis=1
        ).reshape(4, 48, 384)
    start(first_copies(VP))
    swap_f[2] = grad_chunk(group_ids[0], 2)
    swap(2).start()
    att_copy(0).wait_recv()
    att_copy(1).wait_recv()
    swap_f[3] = out_chunk(group_ids[0])
    swap(3).start()
    gim_part[mine, :] = grad_chunk(me, 3)
    ob_part[mine, :] = out_chunk(me)
    small_b[5:6, 0:384] = jnp.sum(grad_qk[...].astype(F32), axis=0, keepdims=True)
    small_b[5:6, 384:576] = jnp.sum(grad_v[...].astype(F32), axis=0, keepdims=True)
    small_b[5:6, 576:768] = jnp.zeros((1, 192), F32)

    def small_copies(number):
        peers = (x_peers, y_peers, [z_pair])[number]
        return [
            copy_to(
                small_r.at[7 + number],
                small_r.at[number * 3 + k],
                small_ss.at[number, k],
                small_rs.at[number, k],
                peers[k],
            )
            for k in range(len(peers))
        ]

    def small_sum(number):
        total = small_r[7 + number]
        for k, item in enumerate(small_copies(number)):
            item.wait_recv()
            total = total + small_r[number * 3 + k]
        return total

    def small_share(k):
        return copy_to(
            small.at[me], small.at[me], small_ss.at[3, k], small_rs.at[3, k], group[k]
        )

    small_r[7] = small_b[...]
    start(small_copies(0))
    first_sum(QK)
    small_r[8] = small_sum(0)
    start(small_copies(1))
    first_sum(VP)
    second_sum(QK)
    small_r[9] = small_sum(1)
    start(small_copies(2))
    second_sum(VP)
    small[me] = small_sum(2)
    for k in range(3):
        small_share(k).start()
    third_sum(QK)
    third_sum(VP)
    start(share_copies(1))

    swap(2).wait_recv()
    far_swap(0).wait_recv()
    values = xx[mine, :].astype(F32)
    center = values - jnp.mean(values, axis=-1, keepdims=True)
    inv_std = lax.rsqrt(jnp.mean(center * center, axis=-1, keepdims=True) + EPSILON)
    norm_rows = center * inv_std
    grad_norm = gim_part[mine, :] + swap_r[2] + far_r[0].astype(F32)
    input_grad[...] = (
        gg[mine, :].astype(F32)
        + inv_std
        * (
            grad_norm
            - jnp.mean(grad_norm, axis=-1, keepdims=True)
            - norm_rows * jnp.mean(grad_norm * norm_rows, axis=-1, keepdims=True)
        )
    ).astype(BF)
    swap(3).wait_recv()
    far_swap(1).wait_recv()
    block_out[...] = (
        values + ob_part[mine, :] + swap_r[3] + far_r[1].astype(F32) + (vec[4:5, :] + vec[5:6, :])
    ).astype(BF)

    share_arrived(0)
    share_arrived(1)
    for k in range(3):
        copy_to(
            small.at[group_ids[k]],
            small.at[group_ids[k]],
            small_ss.at[3, k],
            small_rs.at[3, k],
            group[k],
        ).wait_recv()
    sent = pair + [item for three in tokens for item in three]
    for i in range(N_BLOCK + 1):
        sent += gather(i, 1) + gather(i, 2)
    for i in range(N_BLOCK):
        sent += first_copies(i) + second_copies(i) + [pair_copy(i)]
    sent += p_copies(p_send, p_recv, 0) + p_copies(p_send, p_far, 2, 2) + p_copies(pg_send, pg_recv, 1)
    sent += share_copies(0) + share_copies(1) + [small_share(k) for k in range(3)]
    sent += [swap(k) for k in range(4)] + [far_swap(k) for k in range(2)] + [att_copy(k) for k in range(2)]
    for number in range(3):
        sent += small_copies(number)
    for item in sent:
        item.wait_send()


def whole(x_in, g_in, qkv_weight, proj_weight, up_weight, down_weight, vec_raw, tab):
    shape = jax.ShapeDtypeStruct
    outs = (
        shape((256, WIDTH), BF),
        shape((256, WIDTH), BF),
        shape((4, N_BLOCK, 24, 384), BF),
        shape((4, 8, WIDTH), F32),
    )
    dma = pltpu.SemaphoreType.DMA
    vmem = pl.BlockSpec(memory_space=pltpu.VMEM)
    rows = 1024
    buffers = [
        ((24, 2304), BF),
        ((24, 768), BF),
        ((24, 3072), BF),
        ((96, 768), BF),
        ((8, 128), BF),
        ((3, rows, 128), F32),
        ((N_BLOCK, 24, 384), BF),
        ((16, WIDTH), BF),
        ((N_BLOCK, 4, 4, 48, 384), BF),
        ((4, 4, 16, WIDTH), BF),
        ((N_BLOCK, 24, 384), BF),
        ((16, WIDTH), BF),
        ((16, WIDTH), F32),
        ((rows, WIDTH), BF),
        ((rows, WIDTH), BF),
        ((rows, WIDTH), F32),
        ((rows, WIDTH), BF),
        ((WIDTH, rows), BF),
        ((rows, WIDTH), BF),
        ((WIDTH, rows), BF),
        ((rows, WIDTH), BF),
        ((WIDTH, rows), BF),
        ((rows, WIDTH), F32),
        ((rows, WIDTH), F32),
        ((N_BLOCK, 4, 4, 48, 384), BF),
        ((4, 192, 192), BF),
        ((4, 192, 192), BF),
        ((192, WIDTH), BF),
        ((4, 192, 192), BF),
        ((192, WIDTH), BF),
        ((2, 512, 128), BF),
        ((2, 512, 128), BF),
        ((3, rows, 128), BF),
        ((3, rows, 128), BF),
        ((rows, HEAD_DIM), F32),
        ((rows, HEAD_DIM), F32),
        ((rows, 192), BF),
        ((rows, 384), BF),
        ((rows, 192), BF),
        ((4, 192, 192), BF),
        ((4, 192, 192), BF),
        ((N_BLOCK, 3, 4, 48, 384), BF),
        ((N_BLOCK, 4, 48, 384), BF),
        ((N_BLOCK, 3, 48, 384), BF),
        ((N_BLOCK, 24, 384), F32),
        ((N_BLOCK, 24, 384), BF),
        ((N_BLOCK, 24, 384), BF),
        ((4, 256, WIDTH), F32),
        ((4, 256, WIDTH), F32),
        ((2, 256, WIDTH), BF),
        ((2, 256, WIDTH), BF),
        ((8, WIDTH), F32),
        ((10, 8, WIDTH), F32),
    ]
    sems = [
        (4,),
        (2, 3),
        (N_BLOCK + 1, 3),
        (N_BLOCK + 1, 3),
        (3, 3),
        (N_BLOCK, 3),
        (N_BLOCK, 3),
        (N_BLOCK,),
        (2, 3),
        (8,),
        (4, 3),
    ]
    scratch = [pltpu.VMEM(*item) for item in buffers] + [dma((8,))]
    for item in sems:
        scratch += [dma(item), dma(item)]
    return pl.pallas_call(
        whole_kernel,
        name="whole",
        out_shape=outs,
        in_specs=[pl.BlockSpec(memory_space=pltpu.HBM)] * 8,
        out_specs=(vmem,) * len(outs),
        scratch_shapes=scratch,
        compiler_params=pltpu.CompilerParams(
            collective_id=0, has_side_effects=True, vmem_limit_bytes=60 * MIB
        ),
    )(x_in, g_in, qkv_weight, proj_weight, up_weight, down_weight, vec_raw, tab)


def finish_kernel(
    out_in,
    grad_in,
    owned_in,
    small_in,
    block_out,
    input_grad,
    attn_gain_g,
    attn_bias_g,
    mlp_gain_g,
    mlp_bias_g,
    qkv_g,
    qkv_bias_g,
    proj_g,
    proj_bias_g,
    up_g,
    up_bias_g,
    down_g,
    down_bias_g,
    owned,
    small,
    sems,
):
    copies = [
        pltpu.make_async_copy(owned_in, owned, sems.at[0]),
        pltpu.make_async_copy(small_in, small, sems.at[1]),
        pltpu.make_async_copy(out_in, block_out, sems.at[2]),
        pltpu.make_async_copy(grad_in, input_grad, sems.at[3]),
    ]
    for item in copies:
        item.start()
    copies[0].wait()
    up_parts = []
    for g in range(4):
        qk = owned[g, QK].astype(F32)
        vp = owned[g, VP].astype(F32)
        for head in range(3):
            at = 576 * g + 192 * head
            qkv_g[:, at : at + 128] = qk[:, head * 128 : head * 128 + 128]
            qkv_g[:, at + 128 : at + 192] = vp[:, head * 64 : head * 64 + 64]
        proj_g[:, 192 * g : 192 * g + 192] = vp[:, 192:]
        for half in range(2):
            down_g[24 * g : 24 * g + 24, half * 384 : half * 384 + 384] = owned[
                g, 2 + half
            ].astype(F32)
        up_parts.append([owned[g, 0].astype(F32), owned[g, 1].astype(F32)])
    for d in range(32):
        at = (d % 16) * 24
        up_g[:, 96 * d : 96 * d + 96] = jnp.concatenate(
            [up_parts[g][d // 16][:, at : at + 24] for g in range(4)], axis=1
        )

    copies[1].wait()
    dp = lax.axis_index("dp")
    totals = small[0] + small[1] + small[2] + small[3]
    rows = jnp.concatenate(
        [totals] + [small[g, 6:7, :] for g in range(4)] + [jnp.zeros((4, WIDTH), F32)], axis=0
    )

    def pick(values, each):
        size = values.shape[1]
        row = lax.broadcasted_iota(jnp.int32, (size, each), 0)
        col = lax.broadcasted_iota(jnp.int32, (size, each), 1)
        chosen = (row == col + dp * each).astype(F32)
        return jnp.dot(
            values, chosen, precision=lax.Precision.HIGHEST, preferred_element_type=F32
        )

    picked = pick(rows, 24)
    attn_gain_g[...] = picked[0:1]
    attn_bias_g[...] = picked[1:2]
    mlp_gain_g[...] = picked[2:3]
    mlp_bias_g[...] = picked[3:4]
    proj_bias_g[...] = picked[4:5]
    down_bias_g[...] = picked[4:5]
    up_bias_g[...] = jnp.concatenate([picked[8 + g : 9 + g] for g in range(4)], axis=1)
    pieces = []
    for g in range(4):
        for head in range(3):
            pieces.append(small[g, 5:6, head * 128 : head * 128 + 128])
            pieces.append(small[g, 5:6, 384 + head * 64 : 384 + head * 64 + 64])
    bias = jnp.concatenate(pieces, axis=1)
    qkv_bias_g[...] = pick(jnp.broadcast_to(bias, (8, 2304)), 72)[0:1]
    copies[2].wait()
    copies[3].wait()


def finish(out_in, grad_in, owned, small):
    shape = jax.ShapeDtypeStruct
    outs = (
        shape((256, WIDTH), BF),
        shape((256, WIDTH), BF),
        shape((1, 24), F32),
        shape((1, 24), F32),
        shape((1, 24), F32),
        shape((1, 24), F32),
        shape((24, 2304), F32),
        shape((1, 72), F32),
        shape((24, 768), F32),
        shape((1, 24), F32),
        shape((24, 3072), F32),
        shape((1, 96), F32),
        shape((96, 768), F32),
        shape((1, 24), F32),
    )
    vmem = pl.BlockSpec(memory_space=pltpu.VMEM)
    anywhere = pl.BlockSpec(memory_space=pltpu.HBM)
    return pl.pallas_call(
        finish_kernel,
        name="finish",
        out_shape=outs,
        in_specs=[anywhere] * 4,
        out_specs=(vmem,) * len(outs),
        scratch_shapes=[
            pltpu.VMEM((4, N_BLOCK, 24, 384), BF),
            pltpu.VMEM((4, 8, WIDTH), F32),
            pltpu.SemaphoreType.DMA((4,)),
        ],
        compiler_params=pltpu.CompilerParams(vmem_limit_bytes=60 * MIB),
    )(out_in, grad_in, owned, small)


def rotary_tables():
    half = ROT_DIM // 2
    freqs = np.power(np.float32(10000.0), np.float32(-2.0) * np.arange(half, dtype=np.float32) / np.float32(ROT_DIM))
    angles = np.arange(1024, dtype=np.float32)[:, None] * freqs.astype(np.float32)[None, :]
    cosine, sine = np.cos(angles), np.sin(angles)
    ones = np.ones((1024, HEAD_DIM - ROT_DIM), np.float32)
    zero = np.zeros((1024, half), np.float32)
    cos_row = np.concatenate([cosine, cosine, ones], axis=1)
    left = np.concatenate([-sine, zero, ones * 0.0], axis=1)
    right = np.concatenate([zero, sine, ones * 0.0], axis=1)
    return np.stack([np.tile(t, (1, 2)) for t in (cos_row, left, right)]).astype(np.float32)


def local(
    block_in,
    cotangent,
    attn_gain,
    attn_bias,
    mlp_gain,
    mlp_bias,
    qkv_weight,
    qkv_bias,
    proj_weight,
    proj_bias,
    up_weight,
    up_bias,
    down_weight,
    down_bias,
):
    vec_raw = jnp.zeros((8, 128), BF)
    for row, values in enumerate(
        (attn_gain, attn_bias, mlp_gain, mlp_bias, proj_bias, down_bias, qkv_bias, up_bias)
    ):
        spare = ((row, 7 - row), (0, 128 - values.shape[0]))
        vec_raw = vec_raw + jnp.pad(values[None, :], spare)
    out, grad, owned, small = whole(
        block_in.reshape(256, WIDTH),
        cotangent.reshape(256, WIDTH),
        qkv_weight,
        proj_weight,
        up_weight,
        down_weight,
        vec_raw,
        jnp.asarray(rotary_tables()),
    )
    results = finish(out, grad, owned, small)
    shapes = [(1, 256, WIDTH)] * 2 + [(24,)] * 4
    shapes += [(24, 2304), (72,), (24, 768), (24,), (24, 3072), (96,), (96, 768), (24,)]
    return tuple(value.reshape(size) for value, size in zip(results, shapes))


def solution(mesh):
    tokens = P("dp", "seq", None)
    in_specs = (tokens, tokens) + (P("dp"),) * 4 + (P("dp", None), P("dp")) * 4
    return jax.shard_map(
        local, mesh=mesh, in_specs=in_specs, out_specs=in_specs, check_vma=False
    )
```
